512 devices in a mesh: dp: 8 (over y), seq: 64 (over x, z, core).
Axes of the slice: x: 4, y: 8, z: 8, core: 2. Of those that a mesh axis runs over, the one named last changes fastest.
Arguments:
- tokens: bfloat16 [8, 16384, 512], P('dp', 'seq'), may hold values from -6 to 6
- cotangent: bfloat16 [8, 16384, 512], P('dp', 'seq'), may hold values from -1.25 to 1.25
- up_weight: bfloat16 [512, 2048], P('seq'), may hold values from -0.25 to 0.25
- down_weight: bfloat16 [2048, 512], P('seq'), may hold values from -0.125 to 0.125
- kernel: float32 [31, 512], replicated, may hold values from -1 to 1
- norm_gain: float32 [512], replicated, may hold values from 0.1 to 1.9
- frame_mask: int32 [8, 16384], P('dp', 'seq'), may hold values 0 or 1
- error_memory: float32 [8, 512, 2048], P('dp', 'seq'), may hold values from -6 to 6
- seed_matrix: int32 [2048, 32], replicated, may hold values from -128 to 127
Outputs:
- mixed: bfloat16 [8, 16384, 512], P('dp', 'seq')
- new_memory: float32 [8, 512, 2048], P('dp', 'seq')
- compressed: float32 [512, 2048], P('seq')
The draws below stay inside these ranges and needn't reach their ends.
All inputs are finite; a program needn't handle non-finite values. No bound on the sum of `frame_mask` on one device may be relied on, other than what follows from the above.
Results may differ from the reference program's by a relative error of at most 0.0071.
Values may be sent and summed in bfloat16 or wider, within the bound.
No kernel may reach another device: no remote copies, remote signals or barrier semaphores. Data moves between devices by JAX's collectives and lax.ppermute only.
A program may use at most 64 MiB of HBM per device.

```python
import jax
import jax.numpy as jnp
from jax import lax

D = 512
FF = 2048
KERNEL = 31
RANK = 32
FRAMES = 16384
REPLICAS = 8


def set_ends(array, own_key, least, largest):
    shape = array.shape
    place = [jax.random.randint(jax.random.fold_in(own_key, axis), (), 0, shape[axis]) for axis in range(len(shape))]
    array = array.at[tuple(place)].set(least)
    longest = shape.index(max(shape))
    place[longest] = (place[longest] + 1) % shape[longest]
    return array.at[tuple(place)].set(largest)


def steps_of(key, shape, cuts, least, high):
    gain, own = 1.0, jax.random.fold_in(key, 6)
    for dim, shards_of in cuts:
        steps = jnp.exp(jax.random.uniform(jax.random.fold_in(own, dim), (shards_of,), jnp.float32, least / len(cuts), high / len(cuts)))
        gain = gain * jnp.repeat(steps, shape[dim] // shards_of).reshape([-1 if axis == dim else 1 for axis in range(len(shape))])
    return gain


def gaussian(own_key, shape, width, bound, split=(), held_as=jnp.bfloat16):
    loudness = steps_of(own_key, shape, split, -0.22, 0.18) if split else 1.0
    entries = jax.random.normal(own_key, shape, jnp.float32) * width * loudness
    return jnp.minimum(jnp.maximum(entries, -bound), bound).astype(held_as)


def setup_inputs(seed: int = 0) -> dict:
    seeds = jax.random.split(jax.random.key(seed), 10)
    return {
        "tokens": gaussian(seeds[0], (REPLICAS, FRAMES, D), 1.0, 6.0, ((0, 8), (1, 64))),
        "cotangent": gaussian(seeds[1], (REPLICAS, FRAMES, D), (10.0 * FRAMES ** -0.5), 1.25, ((0, 8), (1, 64))),
        "up_weight": gaussian(seeds[2], (D, FF), D ** -0.5, 0.25, ((0, 64),)),
        "down_weight": gaussian(seeds[3], (FF, D), FF ** -0.5, 0.125, ((0, 64),)),
        "kernel": gaussian(seeds[4], (KERNEL, D), KERNEL ** -0.5, 1.0, (), jnp.float32),
        "norm_gain": jnp.clip(1.0 + 0.18 * jax.random.normal(seeds[5], (D,), jnp.float32), 0.1, 1.9),
        "frame_mask": set_ends((jax.random.randint(seeds[6], (REPLICAS, FRAMES), 0, 2) < 1).astype(jnp.int32), jax.random.fold_in(seeds[6], 1), 0, 1),
        "error_memory": gaussian(seeds[7], (REPLICAS, D, FF), 1.0, 6.0, ((0, 8), (1, 64)), jnp.float32),
        "seed_matrix": set_ends(jax.random.randint(seeds[8], (FF, RANK), -128, 128), jax.random.fold_in(seeds[8], 1), -128, 127).astype(jnp.int32),
    }


def depthwise(sequence, kernel):
    half_width = kernel.shape[0] // 2
    frames = sequence.shape[0]
    widened = jnp.pad(sequence.astype(jnp.float32), ((half_width, half_width), (0, 0)))
    filtered = kernel[0] * widened[0:frames]
    for offset in range(1, kernel.shape[0]):
        filtered = filtered + kernel[offset] * widened[offset:offset + frames]
    return filtered

def layer_norm(stream, norm_gain):
    values = stream.astype(jnp.float32)
    center = lax.optimization_barrier(jnp.mean(values, axis=1, keepdims=True))
    spread = lax.optimization_barrier(jnp.mean((values - center) ** 2, axis=1, keepdims=True))
    return ((values - center) * lax.rsqrt(spread + 1e-05) * norm_gain).astype(jnp.bfloat16)

def one_replica(operands, up_weight, down_weight, kernel, norm_gain):
    sequence, cotangent, frame_mask, error_memory = operands
    filtered = depthwise(sequence, kernel)
    stream = (sequence.astype(jnp.float32) + filtered * jax.nn.sigmoid(filtered)).astype(jnp.bfloat16)
    normed = layer_norm(stream, norm_gain)
    projected = jnp.dot(normed.astype(jnp.float32), up_weight.astype(jnp.float32), preferred_element_type=jnp.float32)
    squashed = jax.nn.sigmoid(projected)
    hidden = (projected * squashed).astype(jnp.bfloat16)
    mixed = (stream.astype(jnp.float32) + 0.5 * jnp.dot(hidden.astype(jnp.float32), down_weight.astype(jnp.float32), preferred_element_type=jnp.float32)).astype(jnp.bfloat16)
    masked = cotangent * frame_mask[:, None].astype(jnp.bfloat16)
    upstream = jnp.dot(masked.astype(jnp.float32), down_weight.T.astype(jnp.float32), preferred_element_type=jnp.float32)
    delta_hidden = (0.5 * upstream * squashed * (1.0 + projected * (1.0 - squashed))).astype(jnp.bfloat16)
    gradient = jnp.dot(normed.T.astype(jnp.float32), delta_hidden.astype(jnp.float32), preferred_element_type=jnp.float32)
    return (mixed, gradient + error_memory)

def reference(tokens, cotangent, up_weight, down_weight, kernel, norm_gain, frame_mask, error_memory, seed_matrix):
    mixed, memory = lax.map(lambda operands: one_replica(operands, up_weight, down_weight, kernel, norm_gain), (tokens, cotangent, frame_mask, error_memory))
    highest = lax.Precision.HIGHEST
    start_matrix = seed_matrix.astype(jnp.float32) / 128.0
    left_factor = lax.optimization_barrier(jnp.sum(jnp.einsum('rdf,fk->rdk', memory, start_matrix, precision=highest), axis=0)) / REPLICAS
    gram_matrix = jnp.dot(left_factor.T, left_factor, precision=highest)
    cholesky_factor = jnp.linalg.cholesky(gram_matrix)
    basis_matrix = jax.scipy.linalg.solve_triangular(cholesky_factor, left_factor.T, lower=True).T
    right_factor = lax.optimization_barrier(jnp.sum(jnp.einsum('rdf,dk->rfk', memory, basis_matrix, precision=highest), axis=0)) / REPLICAS
    compressed = jnp.dot(basis_matrix, right_factor.T, precision=highest)
    new_memory = memory - compressed[None]
    return (mixed, new_memory, compressed)
```

```python
import jax
import jax.numpy as jnp
from jax import lax
from jax.sharding import Mesh
from jax.sharding import PartitionSpec as P

Y, X, Z, C = 8, 4, 8, 2
CHIPS = X * Z
SEQ = ("x", "z", "c")
HIGHEST = lax.Precision.HIGHEST


def halo(block, width):
    count = CHIPS * C
    forward = [(i, i + 1) for i in range(count - 1)]
    backward = [(target, source) for source, target in forward]
    low = lax.ppermute(block[block.shape[0] - width :], SEQ, forward)
    high = lax.ppermute(block[:width], SEQ, backward)
    return low, high


def swap_cores(block):
    return lax.ppermute(block, "c", [(0, 1), (1, 0)])


def layer_norm(stream, norm_gain):
    values = stream.astype(jnp.float32)
    center = jnp.mean(values, axis=1, keepdims=True)
    spread = jnp.mean((values - center) ** 2, axis=1, keepdims=True)
    return ((values - center) * lax.rsqrt(spread + 1e-05) * norm_gain).astype(jnp.bfloat16)


def gather_by_exchange(block, axis):
    copies = jnp.broadcast_to(block[None], (lax.axis_size(axis), *block.shape))
    return lax.all_to_all(copies, axis, 0, 0, tiled=True)


def half_weights(up_weight, down_weight):
    rows, hidden = up_weight.shape
    half = hidden // C
    down_rows, features = down_weight.shape
    moves = []
    for x in range(X):
        for z in range(Z):
            for c in range(C):
                source = (x * Z + z) * C + c
                target = ((2 * (x % 2) + c) * Z + z) * C + x // 2
                moves.append((source, target))
    down_block = lax.ppermute(down_weight, SEQ, moves)
    up_split = up_weight.reshape(rows, C, half).transpose(1, 0, 2)
    up_block = lax.all_to_all(up_split, "c", 0, 0, tiled=True).reshape(C * rows, half)
    packed = jnp.concatenate([up_block[:, :features], up_block[:, features:], down_block], axis=0)
    line = gather_by_exchange(packed, "z")
    whole = gather_by_exchange(line, "x")
    chip_rows = C * rows
    left_part = whole[:, :, :chip_rows].reshape(CHIPS * chip_rows, features)
    right_part = whole[:, :, chip_rows : 2 * chip_rows].reshape(CHIPS * chip_rows, features)
    up_half = jnp.concatenate([left_part, right_part], axis=1)
    down_half = whole[:, :, 2 * chip_rows :].reshape(X // 2, 2, Z, down_rows, features)
    down_half = down_half.transpose(0, 2, 1, 3, 4).reshape(half, features)
    return up_half, down_half


def per_device(
    tokens,
    cotangent,
    up_weight,
    down_weight,
    kernel,
    norm_gain,
    frame_mask,
    error_memory,
    seed_matrix,
):
    half_width = kernel.shape[0] // 2
    frames, features = tokens.shape[1:]
    low, high = halo(tokens[0], half_width)
    masked = cotangent[0] * frame_mask[0][:, None].astype(jnp.bfloat16)
    masked_other = swap_cores(masked)
    up_half, down_half = half_weights(up_weight, down_weight)

    widened = jnp.concatenate([low, tokens[0], high], axis=0).astype(jnp.float32)
    filtered = kernel[0] * widened[0:frames]
    for offset in range(1, kernel.shape[0]):
        filtered = filtered + kernel[offset] * widened[offset : offset + frames]
    stream = (tokens[0].astype(jnp.float32) + filtered * jax.nn.sigmoid(filtered)).astype(
        jnp.bfloat16
    )
    normed = layer_norm(stream, norm_gain)
    normed_other = swap_cores(normed)
    normed_all = jnp.concatenate([normed, normed_other], axis=0)
    masked_all = jnp.concatenate([masked, masked_other], axis=0)
    projected = jnp.dot(normed_all, up_half, preferred_element_type=jnp.float32)
    squashed = jax.nn.sigmoid(projected)
    hidden = (projected * squashed).astype(jnp.bfloat16)
    upstream = lax.dot_general(
        masked_all, down_half, (((1,), (1,)), ((), ())), preferred_element_type=jnp.float32
    )
    delta_hidden = (0.5 * upstream * squashed * (1.0 + projected * (1.0 - squashed))).astype(
        jnp.bfloat16
    )
    grad_part = lax.dot_general(
        normed_all, delta_hidden, (((0,), (0,)), ((), ())), preferred_element_type=jnp.float32
    ).astype(jnp.bfloat16)

    chip_rows = features // CHIPS
    half = grad_part.shape[1]
    pieces = lax.all_to_all(grad_part.reshape(CHIPS, chip_rows, half), ("x", "z"), 0, 0, tiled=True)
    summed = jnp.sum(pieces.astype(jnp.float32), axis=0)

    mixed_part = jnp.dot(hidden, down_half, preferred_element_type=jnp.float32)
    mixed_other = swap_cores(mixed_part[frames:])
    mixed = (stream.astype(jnp.float32) + 0.5 * (mixed_part[:frames] + mixed_other)).astype(
        jnp.bfloat16
    )

    rows = chip_rows // C
    halves = lax.all_to_all(summed.reshape(C, rows, half), "c", 0, 0, tiled=True)
    grad_rows = halves.transpose(1, 0, 2).reshape(rows, C * half)
    memory_rows = grad_rows + error_memory[0]

    chunks = Y * C
    width = memory_rows.shape[1] // chunks
    start_matrix = seed_matrix.astype(jnp.float32) / 128.0
    left_term = jnp.dot(memory_rows, start_matrix, precision=HIGHEST)
    rank = left_term.shape[1]
    by_chunk = memory_rows.reshape(rows, chunks, width).transpose(1, 0, 2)
    message = jnp.concatenate(
        [by_chunk, jnp.broadcast_to(left_term[None], (chunks, rows, rank))], axis=2
    )
    arrived = lax.all_to_all(message, ("y", "c"), 0, 0, tiled=True)
    mean_rows = jnp.sum(arrived.reshape(Y, chip_rows, width + rank), axis=0) / Y
    columns = gather_by_exchange(mean_rows, ("x", "z")).reshape(features, width + rank)
    mean_columns, left_factor = columns[:, :width], columns[:, width:]

    gram_matrix = jnp.dot(left_factor.T, left_factor, precision=HIGHEST)
    cholesky_factor = jnp.linalg.cholesky(gram_matrix)
    basis = jax.scipy.linalg.solve_triangular(cholesky_factor, left_factor.T, lower=True).T
    right_chunk = jnp.dot(mean_columns.T, basis, precision=HIGHEST)
    chip = lax.axis_index(("x", "z"))
    basis_rows = lax.dynamic_slice_in_dim(basis, chip * chip_rows, chip_rows, axis=0)
    piece = jnp.dot(basis_rows, right_chunk.T, precision=HIGHEST)

    piece = jnp.broadcast_to(piece.reshape(1, C, rows, width), (Y, C, rows, width))
    compressed = lax.all_to_all(piece.reshape(chunks, rows, width), ("y", "c"), 0, 0, tiled=True)
    compressed = compressed.transpose(1, 0, 2).reshape(rows, chunks * width)
    new_memory = memory_rows - compressed
    return (mixed[None], new_memory[None], compressed)


def solution(mesh):
    fine = Mesh(mesh.devices.reshape(Y, X, Z, C), ("y", "x", "z", "c"))
    in_specs = (
        P("y", SEQ, None),
        P("y", SEQ, None),
        P(SEQ, None),
        P(SEQ, None),
        P(),
        P(),
        P("y", SEQ),
        P("y", SEQ, None),
        P(),
    )
    out_specs = (P("y", SEQ, None), P("y", SEQ, None), P(SEQ, None))
    return jax.shard_map(
        per_device, mesh=fine, in_specs=in_specs, out_specs=out_specs, check_vma=False
    )
```

```python
import jax
import jax.numpy as jnp
from jax import lax
from jax.experimental import pallas as pl
from jax.experimental.pallas import tpu as pltpu
from jax.sharding import Mesh
from jax.sharding import PartitionSpec as P

Y, X, Z, C = 8, 4, 8, 2
CHIPS = X * Z
RANK = 32
SEQ = ("x", "z", "c")
HIGHEST = lax.Precision.HIGHEST


def halo(block, width):
    count = CHIPS * C
    forward = [(i, i + 1) for i in range(count - 1)]
    backward = [(target, source) for source, target in forward]
    low = lax.ppermute(block[block.shape[0] - width :], SEQ, forward)
    high = lax.ppermute(block[:width], SEQ, backward)
    return low, high


def swap_cores(block):
    return lax.ppermute(block, "c", [(0, 1), (1, 0)])


def layer_norm(stream, norm_gain):
    values = stream.astype(jnp.float32)
    center = jnp.mean(values, axis=1, keepdims=True)
    spread = jnp.mean((values - center) ** 2, axis=1, keepdims=True)
    return ((values - center) * lax.rsqrt(spread + 1e-05) * norm_gain).astype(jnp.bfloat16)


def gather_by_exchange(block, axis):
    copies = jnp.broadcast_to(block[None], (lax.axis_size(axis), *block.shape))
    return lax.all_to_all(copies, axis, 0, 0, tiled=True)


def half_weights(up_weight, down_weight):
    rows, hidden = up_weight.shape
    half = hidden // C
    up_split = up_weight.reshape(rows, C, half).transpose(1, 0, 2)
    up_split = jnp.broadcast_to(up_split[None], (Z, C, rows, half)).reshape(Z * C, rows, half)
    up_line = lax.all_to_all(up_split, ("z", "c"), 0, 0, tiled=True).reshape(Z * C * rows, half)
    up_half = gather_by_exchange(up_line, "x").reshape(X * Z * C * rows, half)

    down_rows, features = down_weight.shape
    down_line = gather_by_exchange(down_weight, ("x", "c")).reshape(X, C * down_rows, features)
    pair = lax.dynamic_slice_in_dim(down_line, lax.axis_index("c") * (X // C), X // C, axis=0)
    down_half = gather_by_exchange(pair, "z").transpose(1, 0, 2, 3).reshape(half, features)
    return up_half, down_half


def top_bits(values):
    return lax.reduce_precision(values, exponent_bits=8, mantissa_bits=7)


def terms(values, count):
    parts = []
    for _ in range(count):
        part = top_bits(values)
        parts.append(part.astype(jnp.bfloat16))
        values = values - part
    return parts


def tail_kernel(chip_ref, columns_ref, piece_ref, rows_scratch):
    width = piece_ref.shape[1]
    rank = RANK
    columns = columns_ref[...].astype(jnp.float32)
    mean_columns = columns[:, :width] + columns[:, width : 2 * width]
    first, second, third = (
        columns[:, 2 * width + rank * i : 2 * width + rank * (i + 1)] for i in range(3)
    )
    left = first + second + third
    left_t = left.T
    gram = jnp.dot(left_t, left, precision=HIGHEST, preferred_element_type=jnp.float32)
    row_index = lax.broadcasted_iota(jnp.int32, (rank, 1), 0)
    solved = left_t
    for k in range(rank):
        scale = lax.rsqrt(gram[k : k + 1, k : k + 1])
        factor = jnp.where(row_index > k, gram[:, k : k + 1] * scale, 0.0)
        gram_row = gram[k : k + 1, :] * scale
        solved_row = solved[k : k + 1, :] * scale
        gram = gram - factor * gram_row
        solved = jnp.where(row_index == k, solved_row, solved - factor * solved_row)
    right_t = jnp.dot(solved, mean_columns, precision=HIGHEST, preferred_element_type=jnp.float32)
    rows_scratch[...] = solved.T
    chip_rows = piece_ref.shape[0]
    basis_rows = rows_scratch[pl.ds(pl.multiple_of(chip_ref[0] * chip_rows, chip_rows), chip_rows), :]
    piece_ref[...] = jnp.dot(
        basis_rows, right_t, precision=HIGHEST, preferred_element_type=jnp.float32
    )


def tail(chip, columns, chip_rows, width):
    features = columns.shape[0]
    return pl.pallas_call(
        tail_kernel,
        out_shape=jax.ShapeDtypeStruct((chip_rows, width), jnp.float32),
        in_specs=[
            pl.BlockSpec(memory_space=pltpu.SMEM),
            pl.BlockSpec(memory_space=pltpu.VMEM),
        ],
        out_specs=pl.BlockSpec(memory_space=pltpu.VMEM),
        scratch_shapes=[pltpu.VMEM((features, RANK), jnp.float32)],
        name="tail",
    )(chip, columns)


def per_device(
    tokens,
    cotangent,
    up_weight,
    down_weight,
    kernel,
    norm_gain,
    frame_mask,
    error_memory,
    seed_matrix,
):
    half_width = kernel.shape[0] // 2
    frames, features = tokens.shape[1:]
    low, high = halo(tokens[0], half_width)
    masked = cotangent[0] * frame_mask[0][:, None].astype(jnp.bfloat16)
    masked_other = swap_cores(masked)
    up_half, down_half = half_weights(up_weight, down_weight)

    widened = jnp.concatenate([low, tokens[0], high], axis=0).astype(jnp.float32)
    filtered = kernel[0] * widened[0:frames]
    for offset in range(1, kernel.shape[0]):
        filtered = filtered + kernel[offset] * widened[offset : offset + frames]
    stream = (tokens[0].astype(jnp.float32) + filtered * jax.nn.sigmoid(filtered)).astype(
        jnp.bfloat16
    )
    normed = layer_norm(stream, norm_gain)
    normed_other = swap_cores(normed)
    normed_all = jnp.concatenate([normed, normed_other], axis=0)
    masked_all = jnp.concatenate([masked, masked_other], axis=0)
    projected = jnp.dot(normed_all, up_half, preferred_element_type=jnp.float32)
    squashed = jax.nn.sigmoid(projected)
    hidden = (projected * squashed).astype(jnp.bfloat16)
    upstream = lax.dot_general(
        masked_all, down_half, (((1,), (1,)), ((), ())), preferred_element_type=jnp.float32
    )
    delta_hidden = (0.5 * upstream * squashed * (1.0 + projected * (1.0 - squashed))).astype(
        jnp.bfloat16
    )
    grad_part = lax.dot_general(
        normed_all, delta_hidden, (((0,), (0,)), ((), ())), preferred_element_type=jnp.float32
    ).astype(jnp.bfloat16)

    half = grad_part.shape[1]
    line_rows = features // X
    rows = line_rows // (Z * C)
    lines = lax.all_to_all(grad_part.reshape(X, line_rows, half), "x", 0, 0, tiled=True)
    line_sum = jnp.sum(lines.astype(jnp.float32), axis=0).reshape(Z * C, rows, half)
    pieces = lax.all_to_all(line_sum, ("z", "c"), 0, 0, tiled=True)
    grad_rows = jnp.sum(pieces.reshape(Z, C, rows, half), axis=0)
    grad_rows = grad_rows.transpose(1, 0, 2).reshape(rows, C * half)
    memory_rows = grad_rows + error_memory[0]

    mixed_part = jnp.dot(hidden, down_half, preferred_element_type=jnp.float32)
    mixed_other = swap_cores(mixed_part[frames:])
    mixed = (stream.astype(jnp.float32) + 0.5 * (mixed_part[:frames] + mixed_other)).astype(
        jnp.bfloat16
    )

    chunks = Y * C
    width = memory_rows.shape[1] // chunks
    chip_rows = C * rows
    start_matrix = seed_matrix.astype(jnp.float32) / 128.0
    left_term = jnp.dot(memory_rows, start_matrix, precision=HIGHEST)
    rank = left_term.shape[1]
    by_chunk = memory_rows.reshape(rows, chunks, width).transpose(1, 0, 2)
    message = jnp.concatenate(
        [by_chunk, jnp.broadcast_to(left_term[None], (chunks, rows, rank))], axis=2
    )
    arrived = lax.all_to_all(message, ("y", "c"), 0, 0, tiled=True)
    mean_rows = jnp.sum(arrived.reshape(Y, chip_rows, width + rank), axis=0) / Y
    packed = jnp.concatenate(
        [
            *terms(mean_rows[:, :width], 2),
            *terms(mean_rows[:, width:], 3),
            jnp.zeros((chip_rows, width - 3 * rank), jnp.bfloat16),
        ],
        axis=1,
    )
    columns = gather_by_exchange(packed, ("x", "z")).reshape(features, packed.shape[1])
    chip = lax.axis_index(("x", "z")).astype(jnp.int32).reshape(1)
    piece = tail(chip, columns, chip_rows, width)

    piece = jnp.broadcast_to(piece.reshape(1, C, rows, width), (Y, C, rows, width))
    compressed = lax.all_to_all(piece.reshape(chunks, rows, width), ("y", "c"), 0, 0, tiled=True)
    compressed = compressed.transpose(1, 0, 2).reshape(rows, chunks * width)
    new_memory = memory_rows - compressed
    return (mixed[None], new_memory[None], compressed)


def solution(mesh):
    fine = Mesh(mesh.devices.reshape(Y, X, Z, C), ("y", "x", "z", "c"))
    in_specs = (
        P("y", SEQ, None),
        P("y", SEQ, None),
        P(SEQ, None),
        P(SEQ, None),
        P(),
        P(),
        P("y", SEQ),
        P("y", SEQ, None),
        P(),
    )
    out_specs = (P("y", SEQ, None), P("y", SEQ, None), P(SEQ, None))
    return jax.shard_map(
        per_device, mesh=fine, in_specs=in_specs, out_specs=out_specs, check_vma=False
    )
```

```python
import jax
import jax.numpy as jnp
from jax import lax
from jax.experimental import pallas as pl
from jax.experimental.pallas import tpu as pltpu
from jax.sharding import Mesh
from jax.sharding import PartitionSpec as P

Y, XH, XL, Z, C = 8, 2, 2, 8, 2
RANK = 32
CHIP = ("xh", "xl", "z")
SEQ = ("xh", "xl", "z", "c")
GROUP = ("xl", "c")
GROUPS = ("xh", "z")
QUARTERS = XL * C
HIGHEST = lax.Precision.HIGHEST


def halo(block, width):
    count = XH * XL * Z * C
    forward = [(i, i + 1) for i in range(count - 1)]
    backward = [(target, source) for source, target in forward]
    low = lax.ppermute(block[block.shape[0] - width :], SEQ, forward)
    high = lax.ppermute(block[:width], SEQ, backward)
    return low, high


def swap(block, axis):
    return lax.ppermute(block, axis, [(0, 1), (1, 0)])


def group_frames(block):
    pair = jnp.stack([block, swap(block, "xl")])
    return jnp.concatenate([pair, swap(pair, "c")]).reshape(-1, block.shape[1])


def layer_norm(stream, norm_gain):
    values = stream.astype(jnp.float32)
    center = jnp.mean(values, axis=1, keepdims=True)
    spread = jnp.mean((values - center) ** 2, axis=1, keepdims=True)
    return ((values - center) * lax.rsqrt(spread + 1e-05) * norm_gain).astype(jnp.bfloat16)


def gather_by_exchange(block, axis):
    copies = jnp.broadcast_to(block[None], (lax.axis_size(axis), *block.shape))
    return lax.all_to_all(copies, axis, 0, 0, tiled=True)


def quarter_weights(up_weight, down_weight):
    rows, hidden = up_weight.shape
    quarter = hidden // QUARTERS
    down_rows, features = down_weight.shape
    moves = []
    for q in range(QUARTERS):
        for z in range(Z):
            for c in range(C):
                source = (q * Z + z) * C + c
                target = ((c * XL + q // C) * Z + z) * C + q % C
                moves.append((source, target))
    down_block = lax.ppermute(down_weight, SEQ, moves)
    up_split = up_weight.reshape(rows, QUARTERS, quarter).transpose(1, 0, 2)
    up_block = lax.all_to_all(up_split, GROUP, 0, 0, tiled=True).reshape(QUARTERS * rows, quarter)
    whole = gather_by_exchange(jnp.concatenate([up_block, down_block], axis=0), GROUPS)
    whole = whole.reshape(XH, Z, QUARTERS * rows + down_rows, features)
    up = whole[:, :, : QUARTERS * rows].reshape(XH, Z, XL, C * rows, quarter)
    up = up.transpose(0, 2, 1, 3, 4).reshape(-1, quarter)
    down = whole[:, :, QUARTERS * rows :].transpose(1, 0, 2, 3).reshape(quarter, features)
    return up, down


def top_bits(values):
    return lax.reduce_precision(values, exponent_bits=8, mantissa_bits=7)


def terms(values, count):
    parts = []
    for _ in range(count):
        part = top_bits(values)
        parts.append(part.astype(jnp.bfloat16))
        values = values - part
    return parts


def tail_kernel(chip_ref, columns_ref, piece_ref, rows_scratch):
    width = piece_ref.shape[1]
    rank = RANK
    columns = columns_ref[...].astype(jnp.float32)
    mean_columns = columns[:, :width] + columns[:, width : 2 * width]
    first, second, third = (
        columns[:, 2 * width + rank * i : 2 * width + rank * (i + 1)] for i in range(3)
    )
    left = first + second + third
    left_t = left.T
    gram = jnp.dot(left_t, left, precision=HIGHEST, preferred_element_type=jnp.float32)
    row_index = lax.broadcasted_iota(jnp.int32, (rank, 1), 0)
    solved = left_t
    for k in range(rank):
        scale = lax.rsqrt(gram[k : k + 1, k : k + 1])
        factor = jnp.where(row_index > k, gram[:, k : k + 1] * scale, 0.0)
        gram_row = gram[k : k + 1, :] * scale
        solved_row = solved[k : k + 1, :] * scale
        gram = gram - factor * gram_row
        solved = jnp.where(row_index == k, solved_row, solved - factor * solved_row)
    right_t = jnp.dot(solved, mean_columns, precision=HIGHEST, preferred_element_type=jnp.float32)
    rows_scratch[...] = solved.T
    chip_rows = piece_ref.shape[0]
    basis_rows = rows_scratch[pl.ds(pl.multiple_of(chip_ref[0] * chip_rows, chip_rows), chip_rows), :]
    piece_ref[...] = jnp.dot(
        basis_rows, right_t, precision=HIGHEST, preferred_element_type=jnp.float32
    )


def tail(chip, columns, chip_rows, width):
    features = columns.shape[0]
    return pl.pallas_call(
        tail_kernel,
        out_shape=jax.ShapeDtypeStruct((chip_rows, width), jnp.float32),
        in_specs=[
            pl.BlockSpec(memory_space=pltpu.SMEM),
            pl.BlockSpec(memory_space=pltpu.VMEM),
        ],
        out_specs=pl.BlockSpec(memory_space=pltpu.VMEM),
        scratch_shapes=[pltpu.VMEM((features, RANK), jnp.float32)],
        name="tail",
    )(chip, columns)


def per_device(
    tokens,
    cotangent,
    up_weight,
    down_weight,
    kernel,
    norm_gain,
    frame_mask,
    error_memory,
    seed_matrix,
):
    half_width = kernel.shape[0] // 2
    frames, features = tokens.shape[1:]
    low, high = halo(tokens[0], half_width)
    masked = cotangent[0] * frame_mask[0][:, None].astype(jnp.bfloat16)
    masked_all = group_frames(masked)
    up, down = quarter_weights(up_weight, down_weight)

    widened = jnp.concatenate([low, tokens[0], high], axis=0).astype(jnp.float32)
    filtered = kernel[0] * widened[0:frames]
    for offset in range(1, kernel.shape[0]):
        filtered = filtered + kernel[offset] * widened[offset : offset + frames]
    stream = (tokens[0].astype(jnp.float32) + filtered * jax.nn.sigmoid(filtered)).astype(
        jnp.bfloat16
    )
    normed = layer_norm(stream, norm_gain)
    normed_all = group_frames(normed)
    projected = jnp.dot(normed_all, up, preferred_element_type=jnp.float32)
    squashed = jax.nn.sigmoid(projected)
    hidden = (projected * squashed).astype(jnp.bfloat16)
    upstream = lax.dot_general(
        masked_all, down, (((1,), (1,)), ((), ())), preferred_element_type=jnp.float32
    )
    delta_hidden = (0.5 * upstream * squashed * (1.0 + projected * (1.0 - squashed))).astype(
        jnp.bfloat16
    )
    grad_part = lax.dot_general(
        normed_all, delta_hidden, (((0,), (0,)), ((), ())), preferred_element_type=jnp.float32
    ).astype(jnp.bfloat16)

    quarter = grad_part.shape[1]
    devices = XH * XL * Z * C
    rows = features // devices
    pieces = lax.all_to_all(grad_part.reshape(devices, rows, quarter), SEQ, 0, 0, tiled=True)
    pieces = pieces.reshape(XH, XL, Z, C, rows, quarter).astype(jnp.float32)
    grad_rows = jnp.sum(pieces, axis=(0, 2)).reshape(QUARTERS, rows, quarter)
    grad_rows = grad_rows.transpose(1, 0, 2).reshape(rows, QUARTERS * quarter)
    memory_rows = grad_rows + error_memory[0]

    mixed_part = jnp.dot(hidden, down, preferred_element_type=jnp.float32)
    mixed_part = mixed_part.reshape(C, XL, frames, features)
    chip_part = mixed_part[0] + swap(mixed_part[1], "c")
    other_chip = swap(chip_part[1].astype(jnp.bfloat16), "xl").astype(jnp.float32)
    mixed = (stream.astype(jnp.float32) + 0.5 * (chip_part[0] + other_chip)).astype(jnp.bfloat16)

    chunks = Y * C
    width = memory_rows.shape[1] // chunks
    chip_rows = C * rows
    start_matrix = seed_matrix.astype(jnp.float32) / 128.0
    left_term = jnp.dot(memory_rows, start_matrix, precision=HIGHEST)
    rank = left_term.shape[1]
    by_chunk = memory_rows.reshape(rows, chunks, width).transpose(1, 0, 2)
    message = jnp.concatenate(
        [by_chunk, jnp.broadcast_to(left_term[None], (chunks, rows, rank))], axis=2
    )
    arrived = lax.all_to_all(message, ("y", "c"), 0, 0, tiled=True)
    mean_rows = jnp.sum(arrived.reshape(Y, chip_rows, width + rank), axis=0) / Y
    packed = jnp.concatenate(
        [
            *terms(mean_rows[:, :width], 2),
            *terms(mean_rows[:, width:], 3),
            jnp.zeros((chip_rows, width - 3 * rank), jnp.bfloat16),
        ],
        axis=1,
    )
    columns = gather_by_exchange(packed, CHIP).reshape(features, packed.shape[1])
    chip = lax.axis_index(CHIP).astype(jnp.int32).reshape(1)
    piece = tail(chip, columns, chip_rows, width)

    piece = jnp.broadcast_to(piece.reshape(1, C, rows, width), (Y, C, rows, width))
    compressed = lax.all_to_all(piece.reshape(chunks, rows, width), ("y", "c"), 0, 0, tiled=True)
    compressed = compressed.transpose(1, 0, 2).reshape(rows, chunks * width)
    new_memory = memory_rows - compressed
    return (mixed[None], new_memory[None], compressed)


def solution(mesh):
    fine = Mesh(mesh.devices.reshape(Y, XH, XL, Z, C), ("y", *SEQ))
    in_specs = (
        P("y", SEQ, None),
        P("y", SEQ, None),
        P(SEQ, None),
        P(SEQ, None),
        P(),
        P(),
        P("y", SEQ),
        P("y", SEQ, None),
        P(),
    )
    out_specs = (P("y", SEQ, None), P("y", SEQ, None), P(SEQ, None))
    return jax.shard_map(
        per_device, mesh=fine, in_specs=in_specs, out_specs=out_specs, check_vma=False
    )
```

```python
import jax
import jax.numpy as jnp
from jax import lax
from jax.experimental import pallas as pl
from jax.experimental.pallas import tpu as pltpu
from jax.sharding import Mesh
from jax.sharding import PartitionSpec as P

Y, XH, XL, Z, C = 8, 2, 2, 8, 2
RANK = 32
CHIP = ("xh", "xl", "z")
SEQ = ("xh", "xl", "z", "c")
GROUP = ("xl", "c")
GROUPS = ("xh", "z")
QUARTERS = XL * C
HIGHEST = lax.Precision.HIGHEST


def halo(block, width):
    count = XH * XL * Z * C
    forward = [(i, i + 1) for i in range(count - 1)]
    backward = [(target, source) for source, target in forward]
    low = lax.ppermute(block[block.shape[0] - width :], SEQ, forward)
    high = lax.ppermute(block[:width], SEQ, backward)
    return low, high


def swap(block, axis):
    return lax.ppermute(block, axis, [(0, 1), (1, 0)])


def group_frames(block):
    pair = jnp.stack([block, swap(block, "xl")])
    return jnp.concatenate([pair, swap(pair, "c")]).reshape(-1, block.shape[1])


def layer_norm(stream, norm_gain):
    values = stream.astype(jnp.float32)
    center = jnp.mean(values, axis=1, keepdims=True)
    spread = jnp.mean((values - center) ** 2, axis=1, keepdims=True)
    return ((values - center) * lax.rsqrt(spread + 1e-05) * norm_gain).astype(jnp.bfloat16)


def gather_by_exchange(block, axis):
    copies = jnp.broadcast_to(block[None], (lax.axis_size(axis), *block.shape))
    return lax.all_to_all(copies, axis, 0, 0, tiled=True)


def quarter_block(up_weight, down_weight):
    rows, hidden = up_weight.shape
    quarter = hidden // QUARTERS
    down_rows, features = down_weight.shape
    moves = []
    for q in range(QUARTERS):
        for z in range(Z):
            for c in range(C):
                source = (q * Z + z) * C + c
                target = ((c * XL + q // C) * Z + z) * C + q % C
                moves.append((source, target))
    down_block = lax.ppermute(down_weight, SEQ, moves)
    up_split = up_weight.reshape(rows, QUARTERS, quarter).transpose(1, 0, 2)
    up_block = lax.all_to_all(up_split, GROUP, 0, 0, tiled=True).reshape(QUARTERS * rows, quarter)
    return jnp.concatenate([up_block, down_block], axis=0)


def quarter_weights(block):
    half, width = block.shape[0] // 2, block.shape[1]
    whole = gather_by_exchange(block, GROUPS).reshape(XH, Z, 2 * half, width)
    up = whole[:, :, :half].reshape(XH, Z, XL, half // XL, width)
    up = up.transpose(0, 2, 1, 3, 4).reshape(-1, width)
    down = whole[:, :, half:].transpose(1, 0, 2, 3).reshape(-1, width)
    return up, down


def top_bits(values):
    return lax.reduce_precision(values, exponent_bits=8, mantissa_bits=7)


def terms(values, count):
    parts = []
    for _ in range(count):
        part = top_bits(values)
        parts.append(part.astype(jnp.bfloat16))
        values = values - part
    return parts


def tail_kernel(chip_ref, columns_ref, message_ref, rows_scratch):
    chunks, rows, width = message_ref.shape
    rank = RANK
    columns = columns_ref[...].astype(jnp.float32)
    mean_columns = columns[:, :width] + columns[:, width : 2 * width]
    first, second, third = (
        columns[:, 2 * width + rank * i : 2 * width + rank * (i + 1)] for i in range(3)
    )
    left = first + second + third
    left_t = left.T
    gram = jnp.dot(left_t, left, precision=HIGHEST, preferred_element_type=jnp.float32)
    row_index = lax.broadcasted_iota(jnp.int32, (rank, 1), 0)
    solved = left_t
    for k in range(rank):
        scale = lax.rsqrt(gram[k : k + 1, k : k + 1])
        factor = jnp.where(row_index > k, gram[:, k : k + 1] * scale, 0.0)
        gram_row = gram[k : k + 1, :] * scale
        solved_row = solved[k : k + 1, :] * scale
        gram = gram - factor * gram_row
        solved = jnp.where(row_index == k, solved_row, solved - factor * solved_row)
    right_t = jnp.dot(solved, mean_columns, precision=HIGHEST, preferred_element_type=jnp.float32)
    rows_scratch[...] = solved.T
    chip_rows = C * rows
    basis_rows = rows_scratch[pl.ds(pl.multiple_of(chip_ref[0] * chip_rows, chip_rows), chip_rows), :]
    piece = jnp.dot(basis_rows, right_t, precision=HIGHEST, preferred_element_type=jnp.float32)
    for chunk in range(chunks):
        half = chunk % C
        message_ref[chunk] = piece[half * rows : (half + 1) * rows]


def tail(chip, columns, chunks, rows, width):
    features = columns.shape[0]
    return pl.pallas_call(
        tail_kernel,
        out_shape=jax.ShapeDtypeStruct((chunks, rows, width), jnp.float32),
        in_specs=[
            pl.BlockSpec(memory_space=pltpu.SMEM),
            pl.BlockSpec(memory_space=pltpu.VMEM),
        ],
        out_specs=pl.BlockSpec(memory_space=pltpu.VMEM),
        scratch_shapes=[pltpu.VMEM((features, RANK), jnp.float32)],
        compiler_params=pltpu.CompilerParams(vmem_limit_bytes=8 * 1024 * 1024),
        name="tail",
    )(chip, columns)


def per_device(
    tokens,
    cotangent,
    up_weight,
    down_weight,
    kernel,
    norm_gain,
    frame_mask,
    error_memory,
    seed_matrix,
):
    half_width = kernel.shape[0] // 2
    frames, features = tokens.shape[1:]
    low, high = halo(tokens[0], half_width)
    masked = cotangent[0] * frame_mask[0][:, None].astype(jnp.bfloat16)
    block = quarter_block(up_weight, down_weight)
    block, masked, low, high = lax.optimization_barrier((block, masked, low, high))
    up, down = quarter_weights(block)
    masked_all = group_frames(masked)

    widened = jnp.concatenate([low, tokens[0], high], axis=0).astype(jnp.float32)
    filtered = kernel[0] * widened[0:frames]
    for offset in range(1, kernel.shape[0]):
        filtered = filtered + kernel[offset] * widened[offset : offset + frames]
    stream = (tokens[0].astype(jnp.float32) + filtered * jax.nn.sigmoid(filtered)).astype(
        jnp.bfloat16
    )
    normed = layer_norm(stream, norm_gain)
    normed_all = group_frames(normed)
    projected = jnp.dot(normed_all, up, preferred_element_type=jnp.float32)
    squashed = jax.nn.sigmoid(projected)
    hidden = (projected * squashed).astype(jnp.bfloat16)
    upstream = lax.dot_general(
        masked_all, down, (((1,), (1,)), ((), ())), preferred_element_type=jnp.float32
    )
    delta_hidden = (0.5 * upstream * squashed * (1.0 + projected * (1.0 - squashed))).astype(
        jnp.bfloat16
    )
    grad_part = lax.dot_general(
        normed_all, delta_hidden, (((0,), (0,)), ((), ())), preferred_element_type=jnp.float32
    ).astype(jnp.bfloat16)

    mixed_part = jnp.dot(hidden, down, preferred_element_type=jnp.float32)
    mixed_part = mixed_part.reshape(C, XL, frames, features)
    chip_part = mixed_part[0] + swap(mixed_part[1], "c")

    quarter = grad_part.shape[1]
    devices = XH * XL * Z * C
    rows = features // devices
    pieces = lax.all_to_all(grad_part.reshape(devices, rows, quarter), SEQ, 0, 0, tiled=True)
    pieces = pieces.reshape(XH, XL, Z, C, rows, quarter).astype(jnp.float32)
    grad_rows = jnp.sum(pieces, axis=(0, 2)).reshape(QUARTERS, rows, quarter)
    grad_rows = grad_rows.transpose(1, 0, 2).reshape(rows, QUARTERS * quarter)
    memory_rows = grad_rows + error_memory[0]

    chunks = Y * C
    width = memory_rows.shape[1] // chunks
    chip_rows = C * rows
    start_matrix = seed_matrix.astype(jnp.float32) / 128.0
    left_term = jnp.dot(memory_rows, start_matrix, precision=HIGHEST)
    rank = left_term.shape[1]
    by_chunk = memory_rows.reshape(rows, chunks, width).transpose(1, 0, 2)
    message = jnp.concatenate(
        [by_chunk, jnp.broadcast_to(left_term[None], (chunks, rows, rank))], axis=2
    )
    message, chip_part = lax.optimization_barrier((message, chip_part))
    other_chip = swap(chip_part[1].astype(jnp.bfloat16), "xl")
    arrived = lax.all_to_all(message, ("y", "c"), 0, 0, tiled=True)
    mean_rows = jnp.sum(arrived.reshape(Y, chip_rows, width + rank), axis=0) / Y
    packed = jnp.concatenate(
        [
            *terms(mean_rows[:, :width], 2),
            *terms(mean_rows[:, width:], 3),
            jnp.zeros((chip_rows, width - 3 * rank), jnp.bfloat16),
        ],
        axis=1,
    )
    packed, other_chip = lax.optimization_barrier((packed, other_chip))
    mixed = (
        stream.astype(jnp.float32) + 0.5 * (chip_part[0] + other_chip.astype(jnp.float32))
    ).astype(jnp.bfloat16)
    columns = gather_by_exchange(packed, CHIP).reshape(features, packed.shape[1])
    chip = lax.axis_index(CHIP).astype(jnp.int32).reshape(1)
    message = tail(chip, columns, chunks, rows, width)
    compressed = lax.all_to_all(message, ("y", "c"), 0, 0, tiled=True)
    compressed = compressed.transpose(1, 0, 2).reshape(rows, chunks * width)
    new_memory = memory_rows - compressed
    return (mixed[None], new_memory[None], compressed)


def solution(mesh):
    fine = Mesh(mesh.devices.reshape(Y, XH, XL, Z, C), ("y", *SEQ))
    in_specs = (
        P("y", SEQ, None),
        P("y", SEQ, None),
        P(SEQ, None),
        P(SEQ, None),
        P(),
        P(),
        P("y", SEQ),
        P("y", SEQ, None),
        P(),
    )
    out_specs = (P("y", SEQ, None), P("y", SEQ, None), P(SEQ, None))
    return jax.shard_map(
        per_device, mesh=fine, in_specs=in_specs, out_specs=out_specs, check_vma=False
    )
```

```python
import jax
import jax.numpy as jnp
from jax import lax
from jax.experimental import pallas as pl
from jax.experimental.pallas import tpu as pltpu
from jax.sharding import Mesh
from jax.sharding import PartitionSpec as P

Y, XH, XL, Z, C = 8, 2, 2, 8, 2
RANK = 32
CHIP = ("xh", "xl", "z")
SEQ = ("xh", "xl", "z", "c")
GROUP = ("xl", "c")
GROUPS = ("xh", "z")
QUARTERS = XL * C
HIGHEST = lax.Precision.HIGHEST


def halo(block, width):
    count = XH * XL * Z * C
    forward = [(i, i + 1) for i in range(count - 1)]
    backward = [(target, source) for source, target in forward]
    low = lax.ppermute(block[block.shape[0] - width :], SEQ, forward)
    high = lax.ppermute(block[:width], SEQ, backward)
    return low, high


def swap(block, axis):
    return lax.ppermute(block, axis, [(0, 1), (1, 0)])


def layer_norm(stream, norm_gain):
    values = stream.astype(jnp.float32)
    center = jnp.mean(values, axis=1, keepdims=True)
    spread = jnp.mean((values - center) ** 2, axis=1, keepdims=True)
    return ((values - center) * lax.rsqrt(spread + 1e-05) * norm_gain).astype(jnp.bfloat16)


def tokens_kernel(
    tokens_ref, low_ref, high_ref, cotangent_ref, mask_ref, taps_ref, gain_ref, stream_ref, pack_ref, wide, held
):
    frames, features = tokens_ref.shape
    edge = low_ref.shape[0]
    taps = taps_ref.shape[0]
    lanes = wide.shape[2]
    for chunk in range(features // lanes):
        columns = slice(chunk * lanes, (chunk + 1) * lanes)
        wide[chunk, :edge] = low_ref[:, columns].astype(jnp.float32)
        wide[chunk, edge : edge + frames] = tokens_ref[:, columns].astype(jnp.float32)
        wide[chunk, edge + frames :] = high_ref[:, columns].astype(jnp.float32)
    block = 64

    @pl.loop(0, frames // block)
    def _(step):
        start = pl.multiple_of(step * block, block)
        for chunk in range(features // lanes):
            columns = slice(chunk * lanes, (chunk + 1) * lanes)
            filtered = None
            for k in range(taps):
                shifted = wide[chunk, pl.ds(start + (edge - taps // 2 + k), block), :]
                term = taps_ref[k : k + 1, columns] * shifted
                filtered = term if filtered is None else filtered + term
            middle = wide[chunk, pl.ds(start + edge, block), :]
            held[pl.ds(start, block), columns] = middle + filtered * jax.nn.sigmoid(filtered)

        stream = held[pl.ds(start, block), :].astype(jnp.bfloat16)
        stream_ref[pl.ds(start, block), :] = stream
        pack_ref[0, pl.ds(start, block), :] = layer_norm(stream, gain_ref[...])

    mask = jnp.broadcast_to(mask_ref[...].astype(jnp.float32), (lanes, frames)).T
    for chunk in range(features // lanes):
        columns = slice(chunk * lanes, (chunk + 1) * lanes)
        masked = cotangent_ref[:, columns].astype(jnp.float32) * mask
        pack_ref[1, :, columns] = masked.astype(jnp.bfloat16)


def tokens_part(tokens, low, high, cotangent, mask, taps, gain):
    frames, features = tokens.shape
    edge = low.shape[0]
    return pl.pallas_call(
        tokens_kernel,
        out_shape=(
            jax.ShapeDtypeStruct((frames, features), jnp.bfloat16),
            jax.ShapeDtypeStruct((2, frames, features), jnp.bfloat16),
        ),
        scratch_shapes=[
            pltpu.VMEM((features // 128, frames + 2 * edge, 128), jnp.float32),
            pltpu.VMEM((frames, features), jnp.float32),
        ],
        compiler_params=pltpu.CompilerParams(vmem_limit_bytes=16 * 1024 * 1024),
        cost_estimate=pl.CostEstimate(flops=8_000_000, bytes_accessed=1_500_000, transcendentals=0),
        name="tokens_part",
    )(tokens, low, high, cotangent, mask, taps, gain)


def hidden_kernel(own_ref, x_ref, c_ref, xc_ref, whole_ref, grad_ref, hidden_ref, down_ref, up, delta):
    half = whole_ref.shape[2] // 2
    part = half // XL
    for xh in range(XH):
        for z in range(Z):
            for xl in range(XL):
                row = ((xh * XL + xl) * Z + z) * part
                up[row : row + part] = whole_ref[xh, z, xl * part : (xl + 1) * part]
            row = (z * XH + xh) * half
            down_ref[row : row + half] = whole_ref[xh, z, half:]
    frames = own_ref.shape[1]
    for index, block in enumerate((own_ref, x_ref, c_ref, xc_ref)):
        rows = slice(index * frames, (index + 1) * frames)
        projected = jnp.dot(block[0], up[...], preferred_element_type=jnp.float32)
        upstream = lax.dot_general(
            block[1], down_ref[...], (((1,), (1,)), ((), ())), preferred_element_type=jnp.float32
        )
        squashed = jax.nn.sigmoid(projected)
        hidden_ref[rows] = (projected * squashed).astype(jnp.bfloat16)
        delta[rows] = (0.5 * upstream * squashed * (1.0 + projected * (1.0 - squashed))).astype(
            jnp.bfloat16
        )
    total = None
    for index, block in enumerate((own_ref, x_ref, c_ref, xc_ref)):
        rows = slice(index * frames, (index + 1) * frames)
        term = lax.dot_general(
            block[0], delta[rows], (((0,), (0,)), ((), ())), preferred_element_type=jnp.float32
        )
        total = term if total is None else total + term
    grad_ref[...] = total.astype(jnp.bfloat16)


def hidden_part(own, x_block, c_block, xc_block, whole):
    frames, features = own.shape[1:]
    quarter = whole.shape[3]
    blocks = XL * C
    return pl.pallas_call(
        hidden_kernel,
        out_shape=(
            jax.ShapeDtypeStruct((features, quarter), jnp.bfloat16),
            jax.ShapeDtypeStruct((blocks * frames, quarter), jnp.bfloat16),
            jax.ShapeDtypeStruct((quarter, features), jnp.bfloat16),
        ),
        scratch_shapes=[
            pltpu.VMEM((features, quarter), jnp.bfloat16),
            pltpu.VMEM((blocks * frames, quarter), jnp.bfloat16),
        ],
        compiler_params=pltpu.CompilerParams(vmem_limit_bytes=32 * 1024 * 1024),
        cost_estimate=pl.CostEstimate(
            flops=6 * blocks * frames * features * quarter, bytes_accessed=6_000_000, transcendentals=0
        ),
        name="hidden_part",
    )(own, x_block, c_block, xc_block, whole)


def gather_by_exchange(block, axis):
    copies = jnp.broadcast_to(block[None], (lax.axis_size(axis), *block.shape))
    return lax.all_to_all(copies, axis, 0, 0, tiled=True)


def quarter_block(up_weight, down_weight):
    rows, hidden = up_weight.shape
    quarter = hidden // QUARTERS
    down_rows, features = down_weight.shape
    moves = []
    for q in range(QUARTERS):
        for z in range(Z):
            for c in range(C):
                source = (q * Z + z) * C + c
                target = ((c * XL + q // C) * Z + z) * C + q % C
                moves.append((source, target))
    down_block = lax.ppermute(down_weight, SEQ, moves)
    up_split = up_weight.reshape(rows, QUARTERS, quarter).transpose(1, 0, 2)
    up_block = lax.all_to_all(up_split, GROUP, 0, 0, tiled=True).reshape(QUARTERS * rows, quarter)
    return jnp.concatenate([up_block, down_block], axis=0)


def top_bits(values):
    return lax.reduce_precision(values, exponent_bits=8, mantissa_bits=7)


def terms(values, count):
    parts = []
    for _ in range(count):
        part = top_bits(values)
        parts.append(part.astype(jnp.bfloat16))
        values = values - part
    return parts


def tail_kernel(chip_ref, columns_ref, message_ref, rows_scratch):
    chunks, rows, width = message_ref.shape
    rank = RANK
    columns = columns_ref[...].astype(jnp.float32)
    mean_columns = columns[:, :width] + columns[:, width : 2 * width]
    first, second, third = (
        columns[:, 2 * width + rank * i : 2 * width + rank * (i + 1)] for i in range(3)
    )
    left = first + second + third
    left_t = left.T
    gram = jnp.dot(left_t, left, precision=HIGHEST, preferred_element_type=jnp.float32)
    row_index = lax.broadcasted_iota(jnp.int32, (rank, 1), 0)
    solved = left_t
    for k in range(rank):
        scale = lax.rsqrt(gram[k : k + 1, k : k + 1])
        factor = jnp.where(row_index > k, gram[:, k : k + 1] * scale, 0.0)
        gram_row = gram[k : k + 1, :] * scale
        solved_row = solved[k : k + 1, :] * scale
        gram = gram - factor * gram_row
        solved = jnp.where(row_index == k, solved_row, solved - factor * solved_row)
    right_t = jnp.dot(solved, mean_columns, precision=HIGHEST, preferred_element_type=jnp.float32)
    rows_scratch[...] = solved.T
    chip_rows = C * rows
    basis_rows = rows_scratch[pl.ds(pl.multiple_of(chip_ref[0] * chip_rows, chip_rows), chip_rows), :]
    piece = jnp.dot(basis_rows, right_t, precision=HIGHEST, preferred_element_type=jnp.float32)
    for chunk in range(chunks):
        half = chunk % C
        message_ref[chunk] = piece[half * rows : (half + 1) * rows]


def tail(chip, columns, chunks, rows, width):
    features = columns.shape[0]
    return pl.pallas_call(
        tail_kernel,
        out_shape=jax.ShapeDtypeStruct((chunks, rows, width), jnp.float32),
        in_specs=[
            pl.BlockSpec(memory_space=pltpu.SMEM),
            pl.BlockSpec(memory_space=pltpu.VMEM),
        ],
        out_specs=pl.BlockSpec(memory_space=pltpu.VMEM),
        scratch_shapes=[pltpu.VMEM((features, RANK), jnp.float32)],
        compiler_params=pltpu.CompilerParams(vmem_limit_bytes=8 * 1024 * 1024),
        name="tail",
    )(chip, columns)


def per_device(
    tokens,
    cotangent,
    up_weight,
    down_weight,
    kernel,
    norm_gain,
    frame_mask,
    error_memory,
    seed_matrix,
):
    frames, features = tokens.shape[1:]
    block = quarter_block(up_weight, down_weight)
    low, high = halo(tokens[0], 16)
    block, low, high = lax.optimization_barrier((block, low, high))
    whole = gather_by_exchange(block, GROUPS).reshape(XH, Z, *block.shape)

    stream, own = tokens_part(
        tokens[0], low, high, cotangent[0], frame_mask, kernel, norm_gain[None]
    )
    x_block = swap(own, "xl")
    c_block = swap(own, "c")
    xc_block = swap(x_block, "c")
    grad_part, hidden, down = hidden_part(own, x_block, c_block, xc_block, whole)

    mixed_part = jnp.dot(hidden, down, preferred_element_type=jnp.float32)
    mixed_part = mixed_part.reshape(C, XL, frames, features)
    chip_part = mixed_part[0] + swap(mixed_part[1], "c")

    quarter = grad_part.shape[1]
    devices = XH * XL * Z * C
    rows = features // devices
    pieces = lax.all_to_all(grad_part.reshape(devices, rows, quarter), SEQ, 0, 0, tiled=True)
    pieces = pieces.reshape(XH, XL, Z, C, rows, quarter).astype(jnp.float32)
    grad_rows = jnp.sum(pieces, axis=(0, 2)).reshape(QUARTERS, rows, quarter)
    grad_rows = grad_rows.transpose(1, 0, 2).reshape(rows, QUARTERS * quarter)
    memory_rows = grad_rows + error_memory[0]

    chunks = Y * C
    width = memory_rows.shape[1] // chunks
    chip_rows = C * rows
    start_matrix = seed_matrix.astype(jnp.float32) / 128.0
    left_term = jnp.dot(memory_rows, start_matrix, precision=HIGHEST)
    rank = left_term.shape[1]
    by_chunk = memory_rows.reshape(rows, chunks, width).transpose(1, 0, 2)
    message = jnp.concatenate(
        [by_chunk, jnp.broadcast_to(left_term[None], (chunks, rows, rank))], axis=2
    )
    message, chip_part = lax.optimization_barrier((message, chip_part))
    other_chip = swap(chip_part[1].astype(jnp.bfloat16), "xl")
    arrived = lax.all_to_all(message, ("y", "c"), 0, 0, tiled=True)
    mean_rows = jnp.sum(arrived.reshape(Y, chip_rows, width + rank), axis=0) / Y
    packed = jnp.concatenate(
        [
            *terms(mean_rows[:, :width], 2),
            *terms(mean_rows[:, width:], 3),
            jnp.zeros((chip_rows, width - 3 * rank), jnp.bfloat16),
        ],
        axis=1,
    )
    packed, other_chip = lax.optimization_barrier((packed, other_chip))
    mixed = (
        stream.astype(jnp.float32) + 0.5 * (chip_part[0] + other_chip.astype(jnp.float32))
    ).astype(jnp.bfloat16)
    columns = gather_by_exchange(packed, CHIP).reshape(features, packed.shape[1])
    chip = lax.axis_index(CHIP).astype(jnp.int32).reshape(1)
    message = tail(chip, columns, chunks, rows, width)
    compressed = lax.all_to_all(message, ("y", "c"), 0, 0, tiled=True)
    compressed = compressed.transpose(1, 0, 2).reshape(rows, chunks * width)
    new_memory = memory_rows - compressed
    return (mixed[None], new_memory[None], compressed)


def solution(mesh):
    fine = Mesh(mesh.devices.reshape(Y, XH, XL, Z, C), ("y", *SEQ))
    in_specs = (
        P("y", SEQ, None),
        P("y", SEQ, None),
        P(SEQ, None),
        P(SEQ, None),
        P(),
        P(),
        P("y", SEQ),
        P("y", SEQ, None),
        P(),
    )
    out_specs = (P("y", SEQ, None), P("y", SEQ, None), P(SEQ, None))
    return jax.shard_map(
        per_device, mesh=fine, in_specs=in_specs, out_specs=out_specs, check_vma=False
    )
```

```python
import jax
import jax.numpy as jnp
from jax import lax
from jax.experimental import pallas as pl
from jax.experimental.pallas import tpu as pltpu
from jax.sharding import Mesh
from jax.sharding import PartitionSpec as P

Y, XH, XL, Z, C = 8, 2, 2, 8, 2
RANK = 32
MASK_ROWS = 16
CHIP = ("xh", "xl", "z")
SEQ = ("xh", "xl", "z", "c")
GROUP = ("xl", "c")
GROUPS = ("xh", "z")
QUARTERS = XL * C
HIGHEST = lax.Precision.HIGHEST


def halo(block, width):
    count = XH * XL * Z * C
    forward = [(i, i + 1) for i in range(count - 1)]
    backward = [(target, source) for source, target in forward]
    low = lax.ppermute(block[block.shape[0] - width :], SEQ, forward)
    high = lax.ppermute(block[:width], SEQ, backward)
    return low, high


def swap(block, axis):
    return lax.ppermute(block, axis, [(0, 1), (1, 0)])


def layer_norm(stream, norm_gain):
    values = stream.astype(jnp.float32)
    center = jnp.mean(values, axis=1, keepdims=True)
    spread = jnp.mean((values - center) ** 2, axis=1, keepdims=True)
    return ((values - center) * lax.rsqrt(spread + 1e-05) * norm_gain).astype(jnp.bfloat16)


def tokens_kernel(
    tokens_ref, low_ref, high_ref, mask_ref, taps_ref, gain_ref, stream_ref, pack_ref, wide, held
):
    frames, features = tokens_ref.shape
    edge = low_ref.shape[0]
    taps = taps_ref.shape[0]
    lanes = wide.shape[2]
    for chunk in range(features // lanes):
        columns = slice(chunk * lanes, (chunk + 1) * lanes)
        wide[chunk, :edge] = low_ref[:, columns].astype(jnp.float32)
        wide[chunk, edge : edge + frames] = tokens_ref[:, columns].astype(jnp.float32)
        wide[chunk, edge + frames :] = high_ref[:, columns].astype(jnp.float32)
    block = 64

    @pl.loop(0, frames // block)
    def _(step):
        start = pl.multiple_of(step * block, block)
        for chunk in range(features // lanes):
            columns = slice(chunk * lanes, (chunk + 1) * lanes)
            filtered = None
            for k in range(taps):
                shifted = wide[chunk, pl.ds(start + (edge - taps // 2 + k), block), :]
                term = taps_ref[k : k + 1, columns] * shifted
                filtered = term if filtered is None else filtered + term
            middle = wide[chunk, pl.ds(start + edge, block), :]
            held[pl.ds(start, block), columns] = middle + filtered * jax.nn.sigmoid(filtered)

        stream = held[pl.ds(start, block), :].astype(jnp.bfloat16)
        stream_ref[pl.ds(start, block), :] = stream
        pack_ref[pl.ds(start, block), :] = layer_norm(stream, gain_ref[...])

    mask = jnp.broadcast_to(mask_ref[...].astype(jnp.float32), (MASK_ROWS, frames))
    pack_ref[frames:, :frames] = mask.astype(jnp.bfloat16)
    pack_ref[frames:, frames:] = jnp.zeros((MASK_ROWS, features - frames), jnp.bfloat16)


def tokens_part(tokens, low, high, mask, taps, gain):
    frames, features = tokens.shape
    edge = low.shape[0]
    return pl.pallas_call(
        tokens_kernel,
        out_shape=(
            jax.ShapeDtypeStruct((frames, features), jnp.bfloat16),
            jax.ShapeDtypeStruct((frames + MASK_ROWS, features), jnp.bfloat16),
        ),
        scratch_shapes=[
            pltpu.VMEM((features // 128, frames + 2 * edge, 128), jnp.float32),
            pltpu.VMEM((frames, features), jnp.float32),
        ],
        compiler_params=pltpu.CompilerParams(vmem_limit_bytes=48 * 1024 * 1024),
        cost_estimate=pl.CostEstimate(flops=8_000_000, bytes_accessed=1_500_000, transcendentals=0),
        name="tokens_part",
    )(tokens, low, high, mask, taps, gain)


def hidden_kernel(
    packs_ref, cotangents_ref, whole_ref, grad_ref, hidden_ref, down_ref, up, delta, masked
):
    half = whole_ref.shape[2] // 2
    part = half // XL
    for xh in range(XH):
        for z in range(Z):
            for xl in range(XL):
                row = ((xh * XL + xl) * Z + z) * part
                up[row : row + part] = whole_ref[xh, z, xl * part : (xl + 1) * part]
            row = (z * XH + xh) * half
            down_ref[row : row + half] = whole_ref[xh, z, half:]
    blocks, frames, features = cotangents_ref.shape
    lanes = 128
    for index in range(blocks):
        rows = slice(index * frames, (index + 1) * frames)
        mask = packs_ref[index, frames:, :frames][:1].astype(jnp.float32)
        mask = jnp.broadcast_to(mask, (lanes, frames)).T
        for chunk in range(features // lanes):
            columns = slice(chunk * lanes, (chunk + 1) * lanes)
            kept = cotangents_ref[index, :, columns].astype(jnp.float32) * mask
            masked[:, columns] = kept.astype(jnp.bfloat16)
        normed = packs_ref[index, :frames]
        projected = jnp.dot(normed, up[...], preferred_element_type=jnp.float32)
        upstream = lax.dot_general(
            masked[...],
            down_ref[...],
            (((1,), (1,)), ((), ())),
            preferred_element_type=jnp.float32,
        )
        squashed = jax.nn.sigmoid(projected)
        hidden_ref[rows] = (projected * squashed).astype(jnp.bfloat16)
        delta[rows] = (0.5 * upstream * squashed * (1.0 + projected * (1.0 - squashed))).astype(
            jnp.bfloat16
        )
    total = None
    for index in range(blocks):
        rows = slice(index * frames, (index + 1) * frames)
        term = lax.dot_general(
            packs_ref[index, :frames],
            delta[rows],
            (((0,), (0,)), ((), ())),
            preferred_element_type=jnp.float32,
        )
        total = term if total is None else total + term
    grad_ref[...] = total.astype(jnp.bfloat16)


def hidden_part(packs, cotangents, whole):
    blocks, frames, features = cotangents.shape
    quarter = whole.shape[3]
    bf16 = jnp.bfloat16
    return pl.pallas_call(
        hidden_kernel,
        out_shape=(
            jax.ShapeDtypeStruct((features, quarter), bf16),
            jax.ShapeDtypeStruct((blocks * frames, quarter), bf16),
            jax.ShapeDtypeStruct((quarter, features), bf16),
        ),
        scratch_shapes=[
            pltpu.VMEM((features, quarter), bf16),
            pltpu.VMEM((blocks * frames, quarter), bf16),
            pltpu.VMEM((frames, features), bf16),
        ],
        compiler_params=pltpu.CompilerParams(vmem_limit_bytes=16 * 1024 * 1024),
        cost_estimate=pl.CostEstimate(
            flops=6 * blocks * frames * features * quarter, bytes_accessed=6_000_000, transcendentals=0
        ),
        name="hidden_part",
    )(packs, cotangents, whole)


def group_frames(block, x_block):
    pair = jnp.stack([block, x_block])
    return jnp.concatenate([pair, swap(pair, "c")])


def gather_by_exchange(block, axis):
    copies = jnp.broadcast_to(block[None], (lax.axis_size(axis), *block.shape))
    return lax.all_to_all(copies, axis, 0, 0, tiled=True)


def quarter_block(up_weight, down_weight):
    rows, hidden = up_weight.shape
    quarter = hidden // QUARTERS
    down_rows, features = down_weight.shape
    moves = []
    for q in range(QUARTERS):
        for z in range(Z):
            for c in range(C):
                source = (q * Z + z) * C + c
                target = ((c * XL + q // C) * Z + z) * C + q % C
                moves.append((source, target))
    down_block = lax.ppermute(down_weight, SEQ, moves)
    up_split = up_weight.reshape(rows, QUARTERS, quarter).transpose(1, 0, 2)
    up_block = lax.all_to_all(up_split, GROUP, 0, 0, tiled=True).reshape(QUARTERS * rows, quarter)
    return jnp.concatenate([up_block, down_block], axis=0)


def top_bits(values):
    return lax.reduce_precision(values, exponent_bits=8, mantissa_bits=7)


def terms(values, count):
    parts = []
    for _ in range(count):
        part = top_bits(values)
        parts.append(part.astype(jnp.bfloat16))
        values = values - part
    return parts


def tail_kernel(chip_ref, columns_ref, message_ref, rows_scratch):
    chunks, rows, width = message_ref.shape
    rank = RANK
    columns = columns_ref[...].astype(jnp.float32)
    mean_columns = columns[:, :width] + columns[:, width : 2 * width]
    first, second, third = (
        columns[:, 2 * width + rank * i : 2 * width + rank * (i + 1)] for i in range(3)
    )
    left = first + second + third
    left_t = left.T
    gram = jnp.dot(left_t, left, precision=HIGHEST, preferred_element_type=jnp.float32)
    row_index = lax.broadcasted_iota(jnp.int32, (rank, 1), 0)
    solved = left_t
    for k in range(rank):
        scale = lax.rsqrt(gram[k : k + 1, k : k + 1])
        factor = jnp.where(row_index > k, gram[:, k : k + 1] * scale, 0.0)
        gram_row = gram[k : k + 1, :] * scale
        solved_row = solved[k : k + 1, :] * scale
        gram = gram - factor * gram_row
        solved = jnp.where(row_index == k, solved_row, solved - factor * solved_row)
    right_t = jnp.dot(solved, mean_columns, precision=HIGHEST, preferred_element_type=jnp.float32)
    rows_scratch[...] = solved.T
    chip_rows = C * rows
    basis_rows = rows_scratch[pl.ds(pl.multiple_of(chip_ref[0] * chip_rows, chip_rows), chip_rows), :]
    piece = jnp.dot(basis_rows, right_t, precision=HIGHEST, preferred_element_type=jnp.float32)
    for chunk in range(chunks):
        half = chunk % C
        message_ref[chunk] = piece[half * rows : (half + 1) * rows]


def tail(chip, columns, chunks, rows, width):
    features = columns.shape[0]
    return pl.pallas_call(
        tail_kernel,
        out_shape=jax.ShapeDtypeStruct((chunks, rows, width), jnp.float32),
        in_specs=[
            pl.BlockSpec(memory_space=pltpu.SMEM),
            pl.BlockSpec(memory_space=pltpu.VMEM),
        ],
        out_specs=pl.BlockSpec(memory_space=pltpu.VMEM),
        scratch_shapes=[pltpu.VMEM((features, RANK), jnp.float32)],
        compiler_params=pltpu.CompilerParams(vmem_limit_bytes=8 * 1024 * 1024),
        name="tail",
    )(chip, columns)


def per_device(
    tokens,
    cotangent,
    up_weight,
    down_weight,
    kernel,
    norm_gain,
    frame_mask,
    error_memory,
    seed_matrix,
):
    frames, features = tokens.shape[1:]
    cotangent_x = swap(cotangent[0], "xl")
    low, high = halo(tokens[0], 16)
    block = quarter_block(up_weight, down_weight)
    block, low, high, cotangent_x = lax.optimization_barrier((block, low, high, cotangent_x))
    whole = gather_by_exchange(block, GROUPS).reshape(XH, Z, *block.shape)
    stream, own = tokens_part(tokens[0], low, high, frame_mask, kernel, norm_gain[None])
    packs = group_frames(own, swap(own, "xl"))
    cotangents = group_frames(cotangent[0], cotangent_x)
    grad_part, hidden, down = hidden_part(packs, cotangents, whole)

    mixed_part = jnp.dot(hidden, down, preferred_element_type=jnp.float32)
    mixed_part = mixed_part.reshape(C, XL, frames, features)
    chip_part = mixed_part[0] + swap(mixed_part[1], "c")

    quarter = grad_part.shape[1]
    devices = XH * XL * Z * C
    rows = features // devices
    pieces = lax.all_to_all(grad_part.reshape(devices, rows, quarter), SEQ, 0, 0, tiled=True)
    pieces = pieces.reshape(XH, XL, Z, C, rows, quarter).astype(jnp.float32)
    grad_rows = jnp.sum(pieces, axis=(0, 2)).reshape(QUARTERS, rows, quarter)
    grad_rows = grad_rows.transpose(1, 0, 2).reshape(rows, QUARTERS * quarter)
    memory_rows = grad_rows + error_memory[0]

    chunks = Y * C
    width = memory_rows.shape[1] // chunks
    chip_rows = C * rows
    start_matrix = seed_matrix.astype(jnp.float32) / 128.0
    left_term = jnp.dot(memory_rows, start_matrix, precision=HIGHEST)
    rank = left_term.shape[1]
    by_chunk = memory_rows.reshape(rows, chunks, width).transpose(1, 0, 2)
    message = jnp.concatenate(
        [by_chunk, jnp.broadcast_to(left_term[None], (chunks, rows, rank))], axis=2
    )
    message, chip_part = lax.optimization_barrier((message, chip_part))
    other_chip = swap(chip_part[1].astype(jnp.bfloat16), "xl")
    arrived = lax.all_to_all(message, ("y", "c"), 0, 0, tiled=True)
    mean_rows = jnp.sum(arrived.reshape(Y, chip_rows, width + rank), axis=0) / Y
    packed = jnp.concatenate(
        [
            *terms(mean_rows[:, :width], 2),
            *terms(mean_rows[:, width:], 3),
            jnp.zeros((chip_rows, width - 3 * rank), jnp.bfloat16),
        ],
        axis=1,
    )
    mixed = (
        stream.astype(jnp.float32) + 0.5 * (chip_part[0] + other_chip.astype(jnp.float32))
    ).astype(jnp.bfloat16)
    columns = gather_by_exchange(packed, CHIP).reshape(features, packed.shape[1])
    chip = lax.axis_index(CHIP).astype(jnp.int32).reshape(1)
    message = tail(chip, columns, chunks, rows, width)
    compressed = lax.all_to_all(message, ("y", "c"), 0, 0, tiled=True)
    compressed = compressed.transpose(1, 0, 2).reshape(rows, chunks * width)
    new_memory = memory_rows - compressed
    return (mixed[None], new_memory[None], compressed)


def solution(mesh):
    fine = Mesh(mesh.devices.reshape(Y, XH, XL, Z, C), ("y", *SEQ))
    in_specs = (
        P("y", SEQ, None),
        P("y", SEQ, None),
        P(SEQ, None),
        P(SEQ, None),
        P(),
        P(),
        P("y", SEQ),
        P("y", SEQ, None),
        P(),
    )
    out_specs = (P("y", SEQ, None), P("y", SEQ, None), P(SEQ, None))
    return jax.shard_map(
        per_device, mesh=fine, in_specs=in_specs, out_specs=out_specs, check_vma=False
    )
```

```python
import jax
import jax.numpy as jnp
from jax import lax
from jax.experimental import pallas as pl
from jax.experimental.pallas import tpu as pltpu
from jax.sharding import Mesh
from jax.sharding import PartitionSpec as P

Y, XH, XL, Z, C = 8, 2, 2, 8, 2
RANK = 32
MASK_ROWS = 16
CHIP = ("xh", "xl", "z")
SEQ = ("xh", "xl", "z", "c")
GROUP = ("xl", "c")
GROUPS = ("xh", "z")
QUARTERS = XL * C
HIGHEST = lax.Precision.HIGHEST


def halo(block, width):
    count = XH * XL * Z * C
    forward = [(i, i + 1) for i in range(count - 1)]
    backward = [(target, source) for source, target in forward]
    low = lax.ppermute(block[block.shape[0] - width :], SEQ, forward)
    high = lax.ppermute(block[:width], SEQ, backward)
    return low, high


def swap(block, axis):
    return lax.ppermute(block, axis, [(0, 1), (1, 0)])


def layer_norm(stream, norm_gain):
    values = stream.astype(jnp.float32)
    center = jnp.mean(values, axis=1, keepdims=True)
    spread = jnp.mean((values - center) ** 2, axis=1, keepdims=True)
    return ((values - center) * lax.rsqrt(spread + 1e-05) * norm_gain).astype(jnp.bfloat16)


def tokens_kernel(
    tokens_ref, low_ref, high_ref, mask_ref, taps_ref, gain_ref, stream_ref, pack_ref, wide, held
):
    frames, features = tokens_ref.shape
    edge = low_ref.shape[0]
    taps = taps_ref.shape[0]
    lanes = wide.shape[2]
    for chunk in range(features // lanes):
        columns = slice(chunk * lanes, (chunk + 1) * lanes)
        wide[chunk, :edge] = low_ref[:, columns].astype(jnp.float32)
        wide[chunk, edge : edge + frames] = tokens_ref[:, columns].astype(jnp.float32)
        wide[chunk, edge + frames :] = high_ref[:, columns].astype(jnp.float32)
    block = 64

    @pl.loop(0, frames // block)
    def _(step):
        start = pl.multiple_of(step * block, block)
        for chunk in range(features // lanes):
            columns = slice(chunk * lanes, (chunk + 1) * lanes)
            filtered = None
            for k in range(taps):
                shifted = wide[chunk, pl.ds(start + (edge - taps // 2 + k), block), :]
                term = taps_ref[k : k + 1, columns] * shifted
                filtered = term if filtered is None else filtered + term
            middle = wide[chunk, pl.ds(start + edge, block), :]
            held[pl.ds(start, block), columns] = middle + filtered * jax.nn.sigmoid(filtered)

        stream = held[pl.ds(start, block), :].astype(jnp.bfloat16)
        stream_ref[pl.ds(start, block), :] = stream
        pack_ref[pl.ds(start, block), :] = layer_norm(stream, gain_ref[...])

    mask = jnp.broadcast_to(mask_ref[...].astype(jnp.float32), (MASK_ROWS, frames))
    pack_ref[frames:, :frames] = mask.astype(jnp.bfloat16)
    pack_ref[frames:, frames:] = jnp.zeros((MASK_ROWS, features - frames), jnp.bfloat16)


def tokens_part(tokens, low, high, mask, taps, gain):
    frames, features = tokens.shape
    edge = low.shape[0]
    return pl.pallas_call(
        tokens_kernel,
        out_shape=(
            jax.ShapeDtypeStruct((frames, features), jnp.bfloat16),
            jax.ShapeDtypeStruct((frames + MASK_ROWS, features), jnp.bfloat16),
        ),
        scratch_shapes=[
            pltpu.VMEM((features // 128, frames + 2 * edge, 128), jnp.float32),
            pltpu.VMEM((frames, features), jnp.float32),
        ],
        compiler_params=pltpu.CompilerParams(vmem_limit_bytes=48 * 1024 * 1024),
        cost_estimate=pl.CostEstimate(flops=8_000_000, bytes_accessed=1_500_000, transcendentals=0),
        name="tokens_part",
    )(tokens, low, high, mask, taps, gain)


def hidden_kernel(
    packs_ref, cotangents_ref, whole_ref, grad_ref, hidden_ref, down_ref, up, delta, masked
):
    half = whole_ref.shape[2] // 2
    part = half // XL
    for xh in range(XH):
        for z in range(Z):
            for xl in range(XL):
                row = ((xh * XL + xl) * Z + z) * part
                up[row : row + part] = whole_ref[xh, z, xl * part : (xl + 1) * part]
            row = (z * XH + xh) * half
            down_ref[row : row + half] = whole_ref[xh, z, half:]
    blocks, frames, features = cotangents_ref.shape
    lanes = 128
    for index in range(blocks):
        rows = slice(index * frames, (index + 1) * frames)
        mask = packs_ref[index, frames:, :frames][:1].astype(jnp.float32)
        mask = jnp.broadcast_to(mask, (lanes, frames)).T
        for chunk in range(features // lanes):
            columns = slice(chunk * lanes, (chunk + 1) * lanes)
            kept = cotangents_ref[index, :, columns].astype(jnp.float32) * mask
            masked[:, columns] = kept.astype(jnp.bfloat16)
        normed = packs_ref[index, :frames]
        projected = jnp.dot(normed, up[...], preferred_element_type=jnp.float32)
        upstream = lax.dot_general(
            masked[...],
            down_ref[...],
            (((1,), (1,)), ((), ())),
            preferred_element_type=jnp.float32,
        )
        squashed = jax.nn.sigmoid(projected)
        hidden_ref[rows] = (projected * squashed).astype(jnp.bfloat16)
        delta[rows] = (0.5 * upstream * squashed * (1.0 + projected * (1.0 - squashed))).astype(
            jnp.bfloat16
        )
    total = None
    for index in range(blocks):
        rows = slice(index * frames, (index + 1) * frames)
        term = lax.dot_general(
            packs_ref[index, :frames],
            delta[rows],
            (((0,), (0,)), ((), ())),
            preferred_element_type=jnp.float32,
        )
        total = term if total is None else total + term
    grad_ref[...] = total.astype(jnp.bfloat16)


def hidden_part(packs, cotangents, whole):
    blocks, frames, features = cotangents.shape
    quarter = whole.shape[3]
    bf16 = jnp.bfloat16
    return pl.pallas_call(
        hidden_kernel,
        out_shape=(
            jax.ShapeDtypeStruct((features, quarter), bf16),
            jax.ShapeDtypeStruct((blocks * frames, quarter), bf16),
            jax.ShapeDtypeStruct((quarter, features), bf16),
        ),
        scratch_shapes=[
            pltpu.VMEM((features, quarter), bf16),
            pltpu.VMEM((blocks * frames, quarter), bf16),
            pltpu.VMEM((frames, features), bf16),
        ],
        compiler_params=pltpu.CompilerParams(vmem_limit_bytes=16 * 1024 * 1024),
        name="hidden_part",
    )(packs, cotangents, whole)


def group_frames(block, x_block):
    pair = jnp.stack([block, x_block])
    return jnp.concatenate([pair, swap(pair, "c")])


def gather_by_exchange(block, axis):
    copies = jnp.broadcast_to(block[None], (lax.axis_size(axis), *block.shape))
    return lax.all_to_all(copies, axis, 0, 0, tiled=True)


def quarter_block(up_weight, down_weight):
    rows, hidden = up_weight.shape
    quarter = hidden // QUARTERS
    down_rows, features = down_weight.shape
    moves = []
    for q in range(QUARTERS):
        for z in range(Z):
            for c in range(C):
                source = (q * Z + z) * C + c
                target = ((c * XL + q // C) * Z + z) * C + q % C
                moves.append((source, target))
    down_block = lax.ppermute(down_weight, SEQ, moves)
    up_split = up_weight.reshape(rows, QUARTERS, quarter).transpose(1, 0, 2)
    up_block = lax.all_to_all(up_split, GROUP, 0, 0, tiled=True).reshape(QUARTERS * rows, quarter)
    return jnp.concatenate([up_block, down_block], axis=0)


def rows_kernel(pieces_ref, error_ref, start_ref, message_ref, memory_ref):
    chips, rows, quarter = pieces_ref.shape
    for xl in range(XL):
        total = None
        for chip in range(chips):
            if chip // Z % XL == xl:
                piece = pieces_ref[chip].astype(jnp.float32)
                total = piece if total is None else total + piece
        columns = slice(xl * quarter, (xl + 1) * quarter)
        memory_ref[:, columns] = total + error_ref[:, columns]
    memory = memory_ref[...]
    left = lax.dot_general(
        memory,
        start_ref[...],
        (((1,), (1,)), ((), ())),
        precision=HIGHEST,
        preferred_element_type=jnp.float32,
    )
    chunks, _, width = message_ref.shape
    part = width // C
    filler = jnp.zeros((rows, width - part - RANK), jnp.float32)
    for chunk in range(chunks):
        columns = slice(chunk * part, (chunk + 1) * part)
        message_ref[chunk] = jnp.concatenate([memory[:, columns], left, filler], axis=1)


def rows_part(pieces, error_rows, start):
    rows, columns = error_rows.shape
    chunks = Y * C
    return pl.pallas_call(
        rows_kernel,
        out_shape=(
            jax.ShapeDtypeStruct((chunks, rows, C * columns // chunks), jnp.float32),
            jax.ShapeDtypeStruct((rows, columns), jnp.float32),
        ),
        compiler_params=pltpu.CompilerParams(vmem_limit_bytes=8 * 1024 * 1024),
        name="rows_part",
    )(pieces, error_rows, start)


def mean_kernel(arrived_ref, message_ref):
    senders, rows, width = arrived_ref.shape
    part = width // C
    sums = []
    for c in range(C):
        total = arrived_ref[c]
        for sender in range(c + C, senders, C):
            total = total + arrived_ref[sender]
        sums.append(total / Y)
    left = sums[0][:, part : part + RANK] + sums[1][:, part : part + RANK]
    parts = [jnp.concatenate([total[:, :part] for total in sums], axis=1).astype(jnp.bfloat16)]
    for _ in range(3):
        parts.append(left.astype(jnp.bfloat16))
        left = left - parts[-1].astype(jnp.float32)
    parts.append(jnp.zeros((rows, width - 3 * RANK), jnp.bfloat16))
    row = jnp.concatenate(parts, axis=1)
    for chip in range(message_ref.shape[0]):
        message_ref[chip] = row


def mean_part(arrived, chips):
    _, rows, width = arrived.shape
    return pl.pallas_call(
        mean_kernel,
        out_shape=jax.ShapeDtypeStruct((chips, rows, 2 * width), jnp.bfloat16),
        compiler_params=pltpu.CompilerParams(vmem_limit_bytes=8 * 1024 * 1024),
        name="mean_part",
    )(arrived)


def last_kernel(arrived_ref, memory_ref, new_ref, compressed_ref):
    chunks, rows, width = arrived_ref.shape
    part = width // C
    per_quarter = chunks // XL
    for xl in range(XL):
        for c in range(C):
            mine = slice(c * part, (c + 1) * part)
            pieces = [arrived_ref[xl * per_quarter + k][:, mine] for k in range(per_quarter)]
            compressed = jnp.concatenate(pieces, axis=1)
            quarter = per_quarter * part
            columns = slice((xl * C + c) * quarter, (xl * C + c + 1) * quarter)
            compressed_ref[:, columns] = compressed
            new_ref[:, columns] = memory_ref[c, :, xl * quarter : (xl + 1) * quarter] - compressed


def last_part(arrived, memory_rows):
    _, rows, columns = memory_rows.shape
    shape = jax.ShapeDtypeStruct((rows, C * columns), jnp.float32)
    return pl.pallas_call(
        last_kernel,
        out_shape=(shape, shape),
        compiler_params=pltpu.CompilerParams(vmem_limit_bytes=8 * 1024 * 1024),
        name="last_part",
    )(arrived, memory_rows)


def by_core(mine, theirs, axis=0):
    first = lax.axis_index("c") == 0
    return jnp.concatenate(
        [jnp.where(first, mine, theirs), jnp.where(first, theirs, mine)], axis=axis
    )


def tail_kernel(chip_ref, columns_ref, message_ref, rows_scratch):
    chunks, rows, width = message_ref.shape
    rank = RANK
    columns = columns_ref[...].astype(jnp.float32)
    mean_columns = columns[:, :width]
    first, second, third = (
        columns[:, width + rank * i : width + rank * (i + 1)] for i in range(3)
    )
    left = first + second + third
    left_t = left.T
    gram = jnp.dot(left_t, left, precision=HIGHEST, preferred_element_type=jnp.float32)
    row_index = lax.broadcasted_iota(jnp.int32, (rank, 1), 0)
    solved = left_t
    for k in range(rank):
        scale = lax.rsqrt(gram[k : k + 1, k : k + 1])
        factor = jnp.where(row_index > k, gram[:, k : k + 1] * scale, 0.0)
        gram_row = gram[k : k + 1, :] * scale
        solved_row = solved[k : k + 1, :] * scale
        gram = gram - factor * gram_row
        solved = jnp.where(row_index == k, solved_row, solved - factor * solved_row)
    right_t = jnp.dot(solved, mean_columns, precision=HIGHEST, preferred_element_type=jnp.float32)
    rows_scratch[...] = solved.T
    chip_rows = C * rows
    basis_rows = rows_scratch[pl.ds(pl.multiple_of(chip_ref[0] * chip_rows, chip_rows), chip_rows), :]
    piece = jnp.dot(basis_rows, right_t, precision=HIGHEST, preferred_element_type=jnp.float32)
    for chunk in range(chunks):
        half = chunk % C
        message_ref[chunk] = piece[half * rows : (half + 1) * rows]


def tail(chip, columns, chunks, rows, width):
    features = columns.shape[0]
    return pl.pallas_call(
        tail_kernel,
        out_shape=jax.ShapeDtypeStruct((chunks, rows, width), jnp.float32),
        in_specs=[
            pl.BlockSpec(memory_space=pltpu.SMEM),
            pl.BlockSpec(memory_space=pltpu.VMEM),
        ],
        out_specs=pl.BlockSpec(memory_space=pltpu.VMEM),
        scratch_shapes=[pltpu.VMEM((features, RANK), jnp.float32)],
        compiler_params=pltpu.CompilerParams(vmem_limit_bytes=8 * 1024 * 1024),
        name="tail",
    )(chip, columns)


def per_device(
    tokens,
    cotangent,
    up_weight,
    down_weight,
    kernel,
    norm_gain,
    frame_mask,
    error_memory,
    seed_matrix,
):
    frames, features = tokens.shape[1:]
    cotangent_x = swap(cotangent[0], "xl")
    low, high = halo(tokens[0], 16)
    block = quarter_block(up_weight, down_weight)
    block, low, high, cotangent_x = lax.optimization_barrier((block, low, high, cotangent_x))
    whole = gather_by_exchange(block, GROUPS).reshape(XH, Z, *block.shape)
    stream, own = tokens_part(tokens[0], low, high, frame_mask, kernel, norm_gain[None])
    packs = group_frames(own, swap(own, "xl"))
    cotangents = group_frames(cotangent[0], cotangent_x)
    grad_part, hidden, down = hidden_part(packs, cotangents, whole)

    mixed_part = jnp.dot(hidden, down, preferred_element_type=jnp.float32)
    mixed_part = mixed_part.reshape(C, XL, frames, features)
    chip_part = mixed_part[0] + swap(mixed_part[1], "c")

    core = lax.axis_index("c")
    rows, quarter = error_memory.shape[1], error_memory.shape[2] // QUARTERS
    error = error_memory[0].reshape(rows, XL, C, quarter).transpose(2, 0, 1, 3)
    error = error.reshape(C, rows, XL * quarter)
    error_rows = by_core(
        lax.dynamic_index_in_dim(error, core, keepdims=False),
        swap(lax.dynamic_index_in_dim(error, 1 - core, keepdims=False), "c"),
    )
    start = (seed_matrix.astype(jnp.float32) / 128.0).T.reshape(RANK, XL, C, quarter)
    start = lax.dynamic_index_in_dim(start, core, axis=2, keepdims=False).reshape(RANK, -1)

    chips = XH * XL * Z
    chip_rows = C * rows
    pieces = lax.all_to_all(grad_part.reshape(chips, chip_rows, quarter), CHIP, 0, 0, tiled=True)
    message, memory = rows_part(pieces, error_rows, start)

    arrived = lax.all_to_all(message, ("y", "c"), 0, 0, tiled=True)
    arrived, memory = lax.optimization_barrier((arrived, memory))
    other_chip = swap(chip_part[1].astype(jnp.bfloat16), "xl")
    mixed = (
        stream.astype(jnp.float32) + 0.5 * (chip_part[0] + other_chip.astype(jnp.float32))
    ).astype(jnp.bfloat16)
    memory = memory.reshape(C, rows, XL * quarter)
    memory_rows = by_core(
        lax.dynamic_index_in_dim(memory, core),
        swap(lax.dynamic_index_in_dim(memory, 1 - core), "c"),
    )
    packed = mean_part(arrived, chips)
    columns = lax.all_to_all(packed, CHIP, 0, 0, tiled=True).reshape(features, -1)
    chip = lax.axis_index(CHIP).astype(jnp.int32).reshape(1)
    width = arrived.shape[2]
    message = tail(chip, columns, Y * C, rows, width)
    arrived = lax.all_to_all(message, ("y", "c"), 0, 0, tiled=True)
    new_memory, compressed = last_part(arrived, memory_rows)
    return (mixed[None], new_memory[None], compressed)


def solution(mesh):
    fine = Mesh(mesh.devices.reshape(Y, XH, XL, Z, C), ("y", *SEQ))
    in_specs = (
        P("y", SEQ, None),
        P("y", SEQ, None),
        P(SEQ, None),
        P(SEQ, None),
        P(),
        P(),
        P("y", SEQ),
        P("y", SEQ, None),
        P(),
    )
    out_specs = (P("y", SEQ, None), P("y", SEQ, None), P(SEQ, None))
    return jax.shard_map(
        per_device, mesh=fine, in_specs=in_specs, out_specs=out_specs, check_vma=False
    )
```

```python
import jax
import jax.numpy as jnp
from jax import lax
from jax.experimental import pallas as pl
from jax.experimental.pallas import tpu as pltpu
from jax.sharding import Mesh
from jax.sharding import PartitionSpec as P

Y, XH, XL, Z, C = 8, 2, 2, 8, 2
RANK = 32
MASK_ROWS = 16
CHIP = ("xh", "xl", "z")
SEQ = ("xh", "xl", "z", "c")
GROUP = ("xl", "c")
GROUPS = ("xh", "z")
QUARTERS = XL * C
HIGHEST = lax.Precision.HIGHEST


def halo(block, width):
    count = XH * XL * Z * C
    forward = [(i, i + 1) for i in range(count - 1)]
    backward = [(target, source) for source, target in forward]
    low = lax.ppermute(block[block.shape[0] - width :], SEQ, forward)
    high = lax.ppermute(block[:width], SEQ, backward)
    return low, high


def swap(block, axis):
    return lax.ppermute(block, axis, [(0, 1), (1, 0)])


def layer_norm(stream, norm_gain):
    values = stream.astype(jnp.float32)
    center = jnp.mean(values, axis=1, keepdims=True)
    spread = jnp.mean((values - center) ** 2, axis=1, keepdims=True)
    return ((values - center) * lax.rsqrt(spread + 1e-05) * norm_gain).astype(jnp.bfloat16)


def tokens_kernel(
    tokens_ref, low_ref, high_ref, mask_ref, taps_ref, gain_ref, stream_ref, pack_ref, wide, held
):
    frames, features = tokens_ref.shape
    edge = low_ref.shape[0]
    taps = taps_ref.shape[0]
    lanes = wide.shape[2]
    for chunk in range(features // lanes):
        columns = slice(chunk * lanes, (chunk + 1) * lanes)
        wide[chunk, :edge] = low_ref[:, columns].astype(jnp.float32)
        wide[chunk, edge : edge + frames] = tokens_ref[:, columns].astype(jnp.float32)
        wide[chunk, edge + frames :] = high_ref[:, columns].astype(jnp.float32)
    block = 64

    @pl.loop(0, frames // block)
    def _(step):
        start = pl.multiple_of(step * block, block)
        for chunk in range(features // lanes):
            columns = slice(chunk * lanes, (chunk + 1) * lanes)
            filtered = None
            for k in range(taps):
                shifted = wide[chunk, pl.ds(start + (edge - taps // 2 + k), block), :]
                term = taps_ref[k : k + 1, columns] * shifted
                filtered = term if filtered is None else filtered + term
            middle = wide[chunk, pl.ds(start + edge, block), :]
            held[pl.ds(start, block), columns] = middle + filtered * jax.nn.sigmoid(filtered)

        stream = held[pl.ds(start, block), :].astype(jnp.bfloat16)
        stream_ref[pl.ds(start, block), :] = stream
        pack_ref[pl.ds(start, block), :] = layer_norm(stream, gain_ref[...])

    mask = jnp.broadcast_to(mask_ref[...].astype(jnp.float32), (MASK_ROWS, frames))
    pack_ref[frames:, :frames] = mask.astype(jnp.bfloat16)
    pack_ref[frames:, frames:] = jnp.zeros((MASK_ROWS, features - frames), jnp.bfloat16)


def tokens_part(tokens, low, high, mask, taps, gain):
    frames, features = tokens.shape
    edge = low.shape[0]
    return pl.pallas_call(
        tokens_kernel,
        out_shape=(
            jax.ShapeDtypeStruct((frames, features), jnp.bfloat16),
            jax.ShapeDtypeStruct((frames + MASK_ROWS, features), jnp.bfloat16),
        ),
        scratch_shapes=[
            pltpu.VMEM((features // 128, frames + 2 * edge, 128), jnp.float32),
            pltpu.VMEM((frames, features), jnp.float32),
        ],
        compiler_params=pltpu.CompilerParams(vmem_limit_bytes=48 * 1024 * 1024),
        cost_estimate=pl.CostEstimate(flops=8_000_000, bytes_accessed=1_500_000, transcendentals=0),
        name="tokens_part",
    )(tokens, low, high, mask, taps, gain)


def hidden_kernel(
    packs_ref, cotangents_ref, whole_ref, grad_ref, both_ref, up, delta, masked
):
    blocks, frames, features = cotangents_ref.shape
    hidden_ref, down_ref = both_ref.at[: blocks * frames], both_ref.at[blocks * frames :]
    half = whole_ref.shape[2] // 2
    part = half // XL
    for xh in range(XH):
        for z in range(Z):
            for xl in range(XL):
                row = ((xh * XL + xl) * Z + z) * part
                up[row : row + part] = whole_ref[xh, z, xl * part : (xl + 1) * part]
            row = (z * XH + xh) * half
            down_ref[row : row + half] = whole_ref[xh, z, half:]
    lanes = 128
    for index in range(blocks):
        rows = slice(index * frames, (index + 1) * frames)
        mask = packs_ref[index, frames:, :frames][:1].astype(jnp.float32)
        mask = jnp.broadcast_to(mask, (lanes, frames)).T
        for chunk in range(features // lanes):
            columns = slice(chunk * lanes, (chunk + 1) * lanes)
            kept = cotangents_ref[index, :, columns].astype(jnp.float32) * mask
            masked[:, columns] = kept.astype(jnp.bfloat16)
        normed = packs_ref[index, :frames]
        projected = jnp.dot(normed, up[...], preferred_element_type=jnp.float32)
        upstream = lax.dot_general(
            masked[...],
            down_ref[...],
            (((1,), (1,)), ((), ())),
            preferred_element_type=jnp.float32,
        )
        squashed = jax.nn.sigmoid(projected)
        hidden_ref[rows] = (projected * squashed).astype(jnp.bfloat16)
        delta[rows] = (0.5 * upstream * squashed * (1.0 + projected * (1.0 - squashed))).astype(
            jnp.bfloat16
        )
    total = None
    for index in range(blocks):
        rows = slice(index * frames, (index + 1) * frames)
        term = lax.dot_general(
            packs_ref[index, :frames],
            delta[rows],
            (((0,), (0,)), ((), ())),
            preferred_element_type=jnp.float32,
        )
        total = term if total is None else total + term
    grad_ref[...] = total.astype(jnp.bfloat16)


def hidden_part(packs, cotangents, whole):
    blocks, frames, features = cotangents.shape
    quarter = whole.shape[3]
    bf16 = jnp.bfloat16
    return pl.pallas_call(
        hidden_kernel,
        out_shape=(
            jax.ShapeDtypeStruct((features, quarter), bf16),
            jax.ShapeDtypeStruct((blocks * frames + quarter, features), bf16),
        ),
        scratch_shapes=[
            pltpu.VMEM((features, quarter), bf16),
            pltpu.VMEM((blocks * frames, quarter), bf16),
            pltpu.VMEM((frames, features), bf16),
        ],
        compiler_params=pltpu.CompilerParams(vmem_limit_bytes=16 * 1024 * 1024),
        name="hidden_part",
    )(packs, cotangents, whole)


def group_frames(block, x_block):
    pair = jnp.stack([block, x_block])
    return jnp.concatenate([pair, swap(pair, "c")])


def gather_by_exchange(block, axis):
    copies = jnp.broadcast_to(block[None], (lax.axis_size(axis), *block.shape))
    return lax.all_to_all(copies, axis, 0, 0, tiled=True)


def quarter_block(up_weight, down_weight):
    rows, hidden = up_weight.shape
    quarter = hidden // QUARTERS
    down_rows, features = down_weight.shape
    moves = []
    for q in range(QUARTERS):
        for z in range(Z):
            for c in range(C):
                source = (q * Z + z) * C + c
                target = ((c * XL + q // C) * Z + z) * C + q % C
                moves.append((source, target))
    down_block = lax.ppermute(down_weight, SEQ, moves)
    up_split = up_weight.reshape(rows, QUARTERS, quarter).transpose(1, 0, 2)
    up_block = lax.all_to_all(up_split, GROUP, 0, 0, tiled=True).reshape(QUARTERS * rows, quarter)
    return jnp.concatenate([up_block, down_block], axis=0)


def rows_kernel(pieces_ref, error_ref, start_ref, error_left_ref, message_ref, grad_ref):
    chips, chip_rows, quarter = pieces_ref.shape
    for xl in range(XL):
        total = None
        for chip in range(chips):
            if chip // Z % XL == xl:
                piece = pieces_ref[chip].astype(jnp.float32)
                total = piece if total is None else total + piece
        grad_ref[:, xl * quarter : (xl + 1) * quarter] = total
    grad = grad_ref[...]
    left = lax.dot_general(
        grad,
        start_ref[...],
        (((1,), (1,)), ((), ())),
        precision=HIGHEST,
        preferred_element_type=jnp.float32,
    )
    rows = error_ref.shape[0]
    error_left = jnp.concatenate(
        [error_left_ref[...], jnp.zeros((chip_rows - rows, RANK), jnp.float32)], axis=0
    )
    chunks, _, width = message_ref.shape
    part = width // C
    for chunk in range(chunks):
        own = slice(chunk * part, (chunk + 1) * part)
        message_ref[chunk, :chip_rows] = jnp.concatenate([grad[:, own], left, error_left], axis=1)
        first = chunk * part // quarter * C * quarter + chunk * part % quarter
        message_ref[chunk, chip_rows:] = jnp.concatenate(
            [error_ref[:, first + c * quarter : first + c * quarter + part] for c in range(C)],
            axis=1,
        )


def rows_part(pieces, error, start, error_left):
    _, chip_rows, quarter = pieces.shape
    rows, columns = error.shape
    chunks = Y * C
    return pl.pallas_call(
        rows_kernel,
        out_shape=(
            jax.ShapeDtypeStruct((chunks, chip_rows + rows, columns // chunks), jnp.float32),
            jax.ShapeDtypeStruct((chip_rows, XL * quarter), jnp.float32),
        ),
        compiler_params=pltpu.CompilerParams(vmem_limit_bytes=8 * 1024 * 1024),
        name="rows_part",
    )(pieces, error, start, error_left)


def mean_kernel(arrived_ref, message_ref):
    senders, _, width = arrived_ref.shape
    chip_rows = message_ref.shape[1]
    rows = chip_rows // C
    part = width // C
    sums = []
    for c in range(C):
        total = arrived_ref[c]
        for sender in range(c + C, senders, C):
            total = total + arrived_ref[sender]
        sums.append(total / Y)
    mean = jnp.concatenate([total[:chip_rows, :part] for total in sums], axis=1)
    mean = mean + jnp.concatenate([total[chip_rows:] for total in sums], axis=0)
    left = sum(total[:chip_rows, part : part + RANK] for total in sums)
    left = left + jnp.concatenate([total[:rows, part + RANK :] for total in sums], axis=0)
    parts = [mean.astype(jnp.bfloat16)]
    for _ in range(3):
        parts.append(left.astype(jnp.bfloat16))
        left = left - parts[-1].astype(jnp.float32)
    parts.append(jnp.zeros((chip_rows, width - 3 * RANK), jnp.bfloat16))
    row = jnp.concatenate(parts, axis=1)
    for chip in range(message_ref.shape[0]):
        message_ref[chip] = row


def mean_part(arrived, chips, chip_rows):
    width = arrived.shape[2]
    return pl.pallas_call(
        mean_kernel,
        out_shape=jax.ShapeDtypeStruct((chips, chip_rows, 2 * width), jnp.bfloat16),
        compiler_params=pltpu.CompilerParams(vmem_limit_bytes=8 * 1024 * 1024),
        name="mean_part",
    )(arrived)


def last_kernel(arrived_ref, grad_ref, error_ref, new_ref, compressed_ref):
    chunks, rows, width = arrived_ref.shape
    part = width // C
    per_quarter = chunks // XL
    for xl in range(XL):
        for c in range(C):
            mine = slice(c * part, (c + 1) * part)
            pieces = [arrived_ref[xl * per_quarter + k][:, mine] for k in range(per_quarter)]
            compressed = jnp.concatenate(pieces, axis=1)
            quarter = per_quarter * part
            columns = slice((xl * C + c) * quarter, (xl * C + c + 1) * quarter)
            compressed_ref[:, columns] = compressed
            memory = grad_ref[c, :, xl * quarter : (xl + 1) * quarter] + error_ref[:, columns]
            new_ref[:, columns] = memory - compressed


def last_part(arrived, grad_rows, error):
    shape = jax.ShapeDtypeStruct(error.shape, jnp.float32)
    return pl.pallas_call(
        last_kernel,
        out_shape=(shape, shape),
        compiler_params=pltpu.CompilerParams(vmem_limit_bytes=8 * 1024 * 1024),
        name="last_part",
    )(arrived, grad_rows, error)


def by_core(mine, theirs, axis=0):
    first = lax.axis_index("c") == 0
    return jnp.concatenate(
        [jnp.where(first, mine, theirs), jnp.where(first, theirs, mine)], axis=axis
    )


def tail_kernel(chip_ref, columns_ref, message_ref, rows_scratch):
    chunks, rows, width = message_ref.shape
    rank = RANK
    columns = columns_ref[...].astype(jnp.float32)
    mean_columns = columns[:, :width]
    first, second, third = (
        columns[:, width + rank * i : width + rank * (i + 1)] for i in range(3)
    )
    left = first + second + third
    left_t = left.T
    gram = jnp.dot(left_t, left, precision=HIGHEST, preferred_element_type=jnp.float32)
    row_index = lax.broadcasted_iota(jnp.int32, (rank, 1), 0)
    solved = left_t
    for k in range(rank):
        scale = lax.rsqrt(gram[k : k + 1, k : k + 1])
        factor = jnp.where(row_index > k, gram[:, k : k + 1] * scale, 0.0)
        gram_row = gram[k : k + 1, :] * scale
        solved_row = solved[k : k + 1, :] * scale
        gram = gram - factor * gram_row
        solved = jnp.where(row_index == k, solved_row, solved - factor * solved_row)
    right_t = jnp.dot(solved, mean_columns, precision=HIGHEST, preferred_element_type=jnp.float32)
    rows_scratch[...] = solved.T
    chip_rows = C * rows
    basis_rows = rows_scratch[pl.ds(pl.multiple_of(chip_ref[0] * chip_rows, chip_rows), chip_rows), :]
    piece = jnp.dot(basis_rows, right_t, precision=HIGHEST, preferred_element_type=jnp.float32)
    for chunk in range(chunks):
        half = chunk % C
        message_ref[chunk] = piece[half * rows : (half + 1) * rows]


def tail(chip, columns, chunks, rows, width):
    features = columns.shape[0]
    return pl.pallas_call(
        tail_kernel,
        out_shape=jax.ShapeDtypeStruct((chunks, rows, width), jnp.float32),
        in_specs=[
            pl.BlockSpec(memory_space=pltpu.SMEM),
            pl.BlockSpec(memory_space=pltpu.VMEM),
        ],
        out_specs=pl.BlockSpec(memory_space=pltpu.VMEM),
        scratch_shapes=[pltpu.VMEM((features, RANK), jnp.float32)],
        compiler_params=pltpu.CompilerParams(vmem_limit_bytes=8 * 1024 * 1024),
        name="tail",
    )(chip, columns)


def per_device(
    tokens,
    cotangent,
    up_weight,
    down_weight,
    kernel,
    norm_gain,
    frame_mask,
    error_memory,
    seed_matrix,
):
    frames, features = tokens.shape[1:]
    cotangent_x = swap(cotangent[0], "xl")
    low, high = halo(tokens[0], 16)
    block = quarter_block(up_weight, down_weight)
    block, low, high, cotangent_x = lax.optimization_barrier((block, low, high, cotangent_x))
    whole = gather_by_exchange(block, GROUPS).reshape(XH, Z, *block.shape)
    stream, own = tokens_part(tokens[0], low, high, frame_mask, kernel, norm_gain[None])
    packs = group_frames(own, swap(own, "xl"))
    cotangents = group_frames(cotangent[0], cotangent_x)
    grad_part, both = hidden_part(packs, cotangents, whole)

    hidden, down = both[: QUARTERS * frames], both[QUARTERS * frames :]
    mixed_part = jnp.dot(hidden, down, preferred_element_type=jnp.float32)
    core = lax.axis_index("c")
    error = error_memory[0]
    rows, quarter = error.shape[0], error.shape[1] // QUARTERS
    start = seed_matrix.astype(jnp.float32) / 128.0
    error_left = jnp.dot(error, start, precision=HIGHEST)
    start = start.T.reshape(RANK, XL, C, quarter)
    start = lax.dynamic_index_in_dim(start, core, axis=2, keepdims=False).reshape(RANK, -1)

    mixed_part = mixed_part.reshape(C, XL, frames, features)
    chip_part = mixed_part[0] + swap(mixed_part[1], "c")

    chips = XH * XL * Z
    chip_rows = C * rows
    pieces = lax.all_to_all(grad_part.reshape(chips, chip_rows, quarter), CHIP, 0, 0, tiled=True)
    message, grad = rows_part(pieces, error, start, error_left)

    arrived = lax.all_to_all(message, ("y", "c"), 0, 0, tiled=True)
    other_chip = swap(chip_part[1].astype(jnp.bfloat16), "xl")
    mixed = (
        stream.astype(jnp.float32) + 0.5 * (chip_part[0] + other_chip.astype(jnp.float32))
    ).astype(jnp.bfloat16)
    grad = grad.reshape(C, rows, XL * quarter)
    grad_rows = by_core(
        lax.dynamic_index_in_dim(grad, core),
        swap(lax.dynamic_index_in_dim(grad, 1 - core), "c"),
    )
    packed = mean_part(arrived, chips, chip_rows)
    columns = lax.all_to_all(packed, CHIP, 0, 0, tiled=True).reshape(features, -1)
    chip = lax.axis_index(CHIP).astype(jnp.int32).reshape(1)
    width = arrived.shape[2]
    message = tail(chip, columns, Y * C, rows, width)
    arrived = lax.all_to_all(message, ("y", "c"), 0, 0, tiled=True)
    new_memory, compressed = last_part(arrived, grad_rows, error)
    return (mixed[None], new_memory[None], compressed)


def solution(mesh):
    fine = Mesh(mesh.devices.reshape(Y, XH, XL, Z, C), ("y", *SEQ))
    in_specs = (
        P("y", SEQ, None),
        P("y", SEQ, None),
        P(SEQ, None),
        P(SEQ, None),
        P(),
        P(),
        P("y", SEQ),
        P("y", SEQ, None),
        P(),
    )
    out_specs = (P("y", SEQ, None), P("y", SEQ, None), P(SEQ, None))
    return jax.shard_map(
        per_device, mesh=fine, in_specs=in_specs, out_specs=out_specs, check_vma=False
    )
```

```python
import jax
import jax.numpy as jnp
from jax import lax
from jax.experimental import pallas as pl
from jax.experimental.pallas import tpu as pltpu
from jax.sharding import Mesh
from jax.sharding import PartitionSpec as P

Y, XH, XL, Z, C = 8, 2, 2, 8, 2
RANK = 32
MASK_ROWS = 16
CHIP = ("xh", "xl", "z")
SEQ = ("xh", "xl", "z", "c")
GROUP = ("xl", "c")
GROUPS = ("xh", "z")
QUARTERS = XL * C
HIGHEST = lax.Precision.HIGHEST


def halo(block, width):
    count = XH * XL * Z * C
    forward = [(i, i + 1) for i in range(count - 1)]
    backward = [(target, source) for source, target in forward]
    low = lax.ppermute(block[block.shape[0] - width :], SEQ, forward)
    high = lax.ppermute(block[:width], SEQ, backward)
    return low, high


def swap(block, axis):
    return lax.ppermute(block, axis, [(0, 1), (1, 0)])


def layer_norm(stream, norm_gain):
    values = stream.astype(jnp.float32)
    center = jnp.mean(values, axis=1, keepdims=True)
    spread = jnp.mean((values - center) ** 2, axis=1, keepdims=True)
    return ((values - center) * lax.rsqrt(spread + 1e-05) * norm_gain).astype(jnp.bfloat16)


def tokens_kernel(
    tokens_ref, low_ref, high_ref, mask_ref, taps_ref, gain_ref, stream_ref, pack_ref, wide, held
):
    frames, features = tokens_ref.shape
    edge = low_ref.shape[0]
    taps = taps_ref.shape[0]
    lanes = wide.shape[2]
    for chunk in range(features // lanes):
        columns = slice(chunk * lanes, (chunk + 1) * lanes)
        wide[chunk, :edge] = low_ref[:, columns].astype(jnp.float32)
        wide[chunk, edge : edge + frames] = tokens_ref[:, columns].astype(jnp.float32)
        wide[chunk, edge + frames :] = high_ref[:, columns].astype(jnp.float32)
    block = 64

    @pl.loop(0, frames // block)
    def _(step):
        start = pl.multiple_of(step * block, block)
        for chunk in range(features // lanes):
            columns = slice(chunk * lanes, (chunk + 1) * lanes)
            filtered = None
            for k in range(taps):
                shifted = wide[chunk, pl.ds(start + (edge - taps // 2 + k), block), :]
                term = taps_ref[k : k + 1, columns] * shifted
                filtered = term if filtered is None else filtered + term
            middle = wide[chunk, pl.ds(start + edge, block), :]
            held[pl.ds(start, block), columns] = middle + filtered * jax.nn.sigmoid(filtered)

        stream = held[pl.ds(start, block), :].astype(jnp.bfloat16)
        stream_ref[pl.ds(start, block), :] = stream
        pack_ref[pl.ds(start, block), :] = layer_norm(stream, gain_ref[...])

    mask = jnp.broadcast_to(mask_ref[...].astype(jnp.float32), (MASK_ROWS, frames))
    pack_ref[frames:, :frames] = mask.astype(jnp.bfloat16)
    pack_ref[frames:, frames:] = jnp.zeros((MASK_ROWS, features - frames), jnp.bfloat16)


def tokens_part(tokens, low, high, mask, taps, gain):
    frames, features = tokens.shape
    edge = low.shape[0]
    return pl.pallas_call(
        tokens_kernel,
        out_shape=(
            jax.ShapeDtypeStruct((frames, features), jnp.bfloat16),
            jax.ShapeDtypeStruct((frames + MASK_ROWS, features), jnp.bfloat16),
        ),
        scratch_shapes=[
            pltpu.VMEM((features // 128, frames + 2 * edge, 128), jnp.float32),
            pltpu.VMEM((frames, features), jnp.float32),
        ],
        compiler_params=pltpu.CompilerParams(vmem_limit_bytes=48 * 1024 * 1024),
        cost_estimate=pl.CostEstimate(flops=8_000_000, bytes_accessed=1_500_000, transcendentals=0),
        name="tokens_part",
    )(tokens, low, high, mask, taps, gain)


def hidden_kernel(
    packs_ref, cotangents_ref, whole_ref, grad_ref, both_ref, up, delta, masked
):
    blocks, frames, features = cotangents_ref.shape
    hidden_ref, down_ref = both_ref.at[: blocks * frames], both_ref.at[blocks * frames :]
    half = whole_ref.shape[2] // 2
    part = half // XL
    for xh in range(XH):
        for z in range(Z):
            for xl in range(XL):
                row = ((xh * XL + xl) * Z + z) * part
                up[row : row + part] = whole_ref[xh, z, xl * part : (xl + 1) * part]
            row = (z * XH + xh) * half
            down_ref[row : row + half] = whole_ref[xh, z, half:]
    lanes = 128
    for index in range(blocks):
        rows = slice(index * frames, (index + 1) * frames)
        mask = packs_ref[index, frames:, :frames][:1].astype(jnp.float32)
        mask = jnp.broadcast_to(mask, (lanes, frames)).T
        for chunk in range(features // lanes):
            columns = slice(chunk * lanes, (chunk + 1) * lanes)
            kept = cotangents_ref[index, :, columns].astype(jnp.float32) * mask
            masked[:, columns] = kept.astype(jnp.bfloat16)
        normed = packs_ref[index, :frames]
        projected = jnp.dot(normed, up[...], preferred_element_type=jnp.float32)
        upstream = lax.dot_general(
            masked[...],
            down_ref[...],
            (((1,), (1,)), ((), ())),
            preferred_element_type=jnp.float32,
        )
        squashed = jax.nn.sigmoid(projected)
        hidden_ref[rows] = (projected * squashed).astype(jnp.bfloat16)
        delta[rows] = (0.5 * upstream * squashed * (1.0 + projected * (1.0 - squashed))).astype(
            jnp.bfloat16
        )
    total = None
    for index in range(blocks):
        rows = slice(index * frames, (index + 1) * frames)
        term = lax.dot_general(
            packs_ref[index, :frames],
            delta[rows],
            (((0,), (0,)), ((), ())),
            preferred_element_type=jnp.float32,
        )
        total = term if total is None else total + term
    grad_ref[...] = total.astype(jnp.bfloat16)


def hidden_part(packs, cotangents, whole):
    blocks, frames, features = cotangents.shape
    quarter = whole.shape[3]
    bf16 = jnp.bfloat16
    return pl.pallas_call(
        hidden_kernel,
        out_shape=(
            jax.ShapeDtypeStruct((features, quarter), bf16),
            jax.ShapeDtypeStruct((blocks * frames + quarter, features), bf16),
        ),
        scratch_shapes=[
            pltpu.VMEM((features, quarter), bf16),
            pltpu.VMEM((blocks * frames, quarter), bf16),
            pltpu.VMEM((frames, features), bf16),
        ],
        compiler_params=pltpu.CompilerParams(vmem_limit_bytes=16 * 1024 * 1024),
        name="hidden_part",
    )(packs, cotangents, whole)


def group_frames(block, x_block):
    pair = jnp.stack([block, x_block])
    return jnp.concatenate([pair, swap(pair, "c")])


def gather_by_exchange(block, axis):
    copies = jnp.broadcast_to(block[None], (lax.axis_size(axis), *block.shape))
    return lax.all_to_all(copies, axis, 0, 0, tiled=True)


def quarter_block(up_weight, down_weight):
    rows, hidden = up_weight.shape
    quarter = hidden // QUARTERS
    down_rows, features = down_weight.shape
    moves = []
    for q in range(QUARTERS):
        for z in range(Z):
            for c in range(C):
                source = (q * Z + z) * C + c
                target = ((c * XL + q // C) * Z + z) * C + q % C
                moves.append((source, target))
    down_block = lax.ppermute(down_weight, SEQ, moves)
    up_split = up_weight.reshape(rows, QUARTERS, quarter).transpose(1, 0, 2)
    up_block = lax.all_to_all(up_split, GROUP, 0, 0, tiled=True).reshape(QUARTERS * rows, quarter)
    return jnp.concatenate([up_block, down_block], axis=0)


def rows_kernel(pieces_ref, error_ref, start_ref, message_ref, memory_ref):
    chips, rows, quarter = pieces_ref.shape
    for xl in range(XL):
        total = None
        for chip in range(chips):
            if chip // Z % XL == xl:
                piece = pieces_ref[chip].astype(jnp.float32)
                total = piece if total is None else total + piece
        columns = slice(xl * quarter, (xl + 1) * quarter)
        memory_ref[:, columns] = total + error_ref[:, columns]
    memory = memory_ref[...]
    left = lax.dot_general(
        memory,
        start_ref[...],
        (((1,), (1,)), ((), ())),
        precision=HIGHEST,
        preferred_element_type=jnp.float32,
    )
    chunks, _, width = message_ref.shape
    part = width // C
    high = left.astype(jnp.bfloat16)
    low = (left - high.astype(jnp.float32)).astype(jnp.bfloat16)
    kept = memory.astype(jnp.bfloat16)
    for chunk in range(chunks):
        columns = slice(chunk * part, (chunk + 1) * part)
        message_ref[chunk] = jnp.concatenate([kept[:, columns], high, low], axis=1)


def rows_part(pieces, error_rows, start):
    rows, columns = error_rows.shape
    chunks = Y * C
    return pl.pallas_call(
        rows_kernel,
        out_shape=(
            jax.ShapeDtypeStruct((chunks, rows, C * columns // chunks), jnp.bfloat16),
            jax.ShapeDtypeStruct((rows, columns), jnp.float32),
        ),
        compiler_params=pltpu.CompilerParams(vmem_limit_bytes=8 * 1024 * 1024),
        name="rows_part",
    )(pieces, error_rows, start)


def mean_kernel(arrived_ref, message_ref):
    senders, rows, width = arrived_ref.shape
    part = width // C
    sums = []
    for c in range(C):
        total = arrived_ref[c].astype(jnp.float32)
        for sender in range(c + C, senders, C):
            total = total + arrived_ref[sender].astype(jnp.float32)
        sums.append(total / Y)
    left = sum(total[:, part : part + RANK] + total[:, part + RANK :] for total in sums)
    parts = [jnp.concatenate([total[:, :part] for total in sums], axis=1).astype(jnp.bfloat16)]
    for _ in range(3):
        parts.append(left.astype(jnp.bfloat16))
        left = left - parts[-1].astype(jnp.float32)
    parts.append(jnp.zeros((rows, width - 3 * RANK), jnp.bfloat16))
    row = jnp.concatenate(parts, axis=1)
    for chip in range(message_ref.shape[0]):
        message_ref[chip] = row


def mean_part(arrived, chips):
    _, rows, width = arrived.shape
    return pl.pallas_call(
        mean_kernel,
        out_shape=jax.ShapeDtypeStruct((chips, rows, 2 * width), jnp.bfloat16),
        compiler_params=pltpu.CompilerParams(vmem_limit_bytes=8 * 1024 * 1024),
        name="mean_part",
    )(arrived)


def last_kernel(arrived_ref, memory_ref, new_ref, compressed_ref):
    chunks, rows, width = arrived_ref.shape
    part = width // C
    per_quarter = chunks // XL
    for xl in range(XL):
        for c in range(C):
            mine = slice(c * part, (c + 1) * part)
            pieces = [arrived_ref[xl * per_quarter + k][:, mine] for k in range(per_quarter)]
            compressed = jnp.concatenate(pieces, axis=1)
            quarter = per_quarter * part
            columns = slice((xl * C + c) * quarter, (xl * C + c + 1) * quarter)
            compressed_ref[:, columns] = compressed
            new_ref[:, columns] = memory_ref[c, :, xl * quarter : (xl + 1) * quarter] - compressed


def last_part(arrived, memory_rows):
    _, rows, columns = memory_rows.shape
    shape = jax.ShapeDtypeStruct((rows, C * columns), jnp.float32)
    return pl.pallas_call(
        last_kernel,
        out_shape=(shape, shape),
        compiler_params=pltpu.CompilerParams(vmem_limit_bytes=8 * 1024 * 1024),
        name="last_part",
    )(arrived, memory_rows)


def by_core(mine, theirs, axis=0):
    first = lax.axis_index("c") == 0
    return jnp.concatenate(
        [jnp.where(first, mine, theirs), jnp.where(first, theirs, mine)], axis=axis
    )


def tail_kernel(chip_ref, columns_ref, message_ref, rows_scratch):
    chunks, rows, width = message_ref.shape
    rank = RANK
    columns = columns_ref[...].astype(jnp.float32)
    mean_columns = columns[:, :width]
    first, second, third = (
        columns[:, width + rank * i : width + rank * (i + 1)] for i in range(3)
    )
    left = first + second + third
    left_t = left.T
    gram = jnp.dot(left_t, left, precision=HIGHEST, preferred_element_type=jnp.float32)
    row_index = lax.broadcasted_iota(jnp.int32, (rank, 1), 0)
    solved = left_t
    for k in range(rank):
        scale = lax.rsqrt(gram[k : k + 1, k : k + 1])
        factor = jnp.where(row_index > k, gram[:, k : k + 1] * scale, 0.0)
        gram_row = gram[k : k + 1, :] * scale
        solved_row = solved[k : k + 1, :] * scale
        gram = gram - factor * gram_row
        solved = jnp.where(row_index == k, solved_row, solved - factor * solved_row)
    right_t = jnp.dot(solved, mean_columns, precision=HIGHEST, preferred_element_type=jnp.float32)
    rows_scratch[...] = solved.T
    chip_rows = C * rows
    basis_rows = rows_scratch[pl.ds(pl.multiple_of(chip_ref[0] * chip_rows, chip_rows), chip_rows), :]
    piece = jnp.dot(basis_rows, right_t, precision=HIGHEST, preferred_element_type=jnp.float32)
    for chunk in range(chunks):
        half = chunk % C
        message_ref[chunk] = piece[half * rows : (half + 1) * rows]


def tail(chip, columns, chunks, rows, width):
    features = columns.shape[0]
    return pl.pallas_call(
        tail_kernel,
        out_shape=jax.ShapeDtypeStruct((chunks, rows, width), jnp.float32),
        in_specs=[
            pl.BlockSpec(memory_space=pltpu.SMEM),
            pl.BlockSpec(memory_space=pltpu.VMEM),
        ],
        out_specs=pl.BlockSpec(memory_space=pltpu.VMEM),
        scratch_shapes=[pltpu.VMEM((features, RANK), jnp.float32)],
        compiler_params=pltpu.CompilerParams(vmem_limit_bytes=8 * 1024 * 1024),
        name="tail",
    )(chip, columns)


def per_device(
    tokens,
    cotangent,
    up_weight,
    down_weight,
    kernel,
    norm_gain,
    frame_mask,
    error_memory,
    seed_matrix,
):
    frames, features = tokens.shape[1:]
    cotangent_x = swap(cotangent[0], "xl")
    low, high = halo(tokens[0], 16)
    block = quarter_block(up_weight, down_weight)
    block, low, high, cotangent_x = lax.optimization_barrier((block, low, high, cotangent_x))
    whole = gather_by_exchange(block, GROUPS).reshape(XH, Z, *block.shape)
    stream, own = tokens_part(tokens[0], low, high, frame_mask, kernel, norm_gain[None])
    packs = group_frames(own, swap(own, "xl"))
    cotangents = group_frames(cotangent[0], cotangent_x)
    grad_part, both = hidden_part(packs, cotangents, whole)

    hidden, down = both[: QUARTERS * frames], both[QUARTERS * frames :]
    mixed_part = jnp.dot(hidden, down, preferred_element_type=jnp.float32)
    mixed_part = mixed_part.reshape(C, XL, frames, features)
    mixed_away, error = lax.optimization_barrier((mixed_part[1], error_memory[0]))
    chip_part = mixed_part[0] + swap(mixed_away, "c")

    core = lax.axis_index("c")
    rows, quarter = error.shape[0], error.shape[1] // QUARTERS
    error = error.reshape(rows, XL, C, quarter).transpose(2, 0, 1, 3)
    error = error.reshape(C, rows, XL * quarter)
    error_rows = by_core(
        lax.dynamic_index_in_dim(error, core, keepdims=False),
        swap(lax.dynamic_index_in_dim(error, 1 - core, keepdims=False), "c"),
    )
    start = (seed_matrix.astype(jnp.float32) / 128.0).T.reshape(RANK, XL, C, quarter)
    start = lax.dynamic_index_in_dim(start, core, axis=2, keepdims=False).reshape(RANK, -1)

    chips = XH * XL * Z
    chip_rows = C * rows
    pieces = lax.all_to_all(grad_part.reshape(chips, chip_rows, quarter), CHIP, 0, 0, tiled=True)
    message, memory = rows_part(pieces, error_rows, start)

    arrived = lax.all_to_all(message, ("y", "c"), 0, 0, tiled=True)
    other_chip = swap(chip_part[1].astype(jnp.bfloat16), "xl")
    mixed = (
        stream.astype(jnp.float32) + 0.5 * (chip_part[0] + other_chip.astype(jnp.float32))
    ).astype(jnp.bfloat16)
    memory = memory.reshape(C, rows, XL * quarter)
    memory_rows = by_core(
        lax.dynamic_index_in_dim(memory, core),
        swap(lax.dynamic_index_in_dim(memory, 1 - core), "c"),
    )
    packed = mean_part(arrived, chips)
    columns = lax.all_to_all(packed, CHIP, 0, 0, tiled=True).reshape(features, -1)
    chip = lax.axis_index(CHIP).astype(jnp.int32).reshape(1)
    width = arrived.shape[2]
    message = tail(chip, columns, Y * C, rows, width)
    arrived = lax.all_to_all(message, ("y", "c"), 0, 0, tiled=True)
    new_memory, compressed = last_part(arrived, memory_rows)
    return (mixed[None], new_memory[None], compressed)


def solution(mesh):
    fine = Mesh(mesh.devices.reshape(Y, XH, XL, Z, C), ("y", *SEQ))
    in_specs = (
        P("y", SEQ, None),
        P("y", SEQ, None),
        P(SEQ, None),
        P(SEQ, None),
        P(),
        P(),
        P("y", SEQ),
        P("y", SEQ, None),
        P(),
    )
    out_specs = (P("y", SEQ, None), P("y", SEQ, None), P(SEQ, None))
    return jax.shard_map(
        per_device, mesh=fine, in_specs=in_specs, out_specs=out_specs, check_vma=False
    )
```

```python
import jax
import jax.numpy as jnp
from jax import lax
from jax.experimental import pallas as pl
from jax.experimental.pallas import tpu as pltpu
from jax.sharding import Mesh
from jax.sharding import PartitionSpec as P

Y, XH, XL, Z, C = 8, 2, 2, 8, 2
RANK = 32
MASK_ROWS = 16
CHIP = ("xh", "xl", "z")
SEQ = ("xh", "xl", "z", "c")
GROUP = ("xl", "c")
GROUPS = ("xh", "z")
QUARTERS = XL * C
HIGHEST = lax.Precision.HIGHEST


def halo(block, width):
    count = XH * XL * Z * C
    forward = [(i, i + 1) for i in range(count - 1)]
    backward = [(target, source) for source, target in forward]
    low = lax.ppermute(block[block.shape[0] - width :], SEQ, forward)
    high = lax.ppermute(block[:width], SEQ, backward)
    return low, high


def swap(block, axis):
    return lax.ppermute(block, axis, [(0, 1), (1, 0)])


def layer_norm(stream, norm_gain):
    values = stream.astype(jnp.float32)
    center = jnp.mean(values, axis=1, keepdims=True)
    spread = jnp.mean((values - center) ** 2, axis=1, keepdims=True)
    return ((values - center) * lax.rsqrt(spread + 1e-05) * norm_gain).astype(jnp.bfloat16)


def tokens_kernel(
    tokens_ref, low_ref, high_ref, mask_ref, taps_ref, gain_ref, stream_ref, pack_ref, wide, held
):
    frames, features = tokens_ref.shape
    edge = low_ref.shape[0]
    taps = taps_ref.shape[0]
    lanes = wide.shape[2]
    for chunk in range(features // lanes):
        columns = slice(chunk * lanes, (chunk + 1) * lanes)
        wide[chunk, :edge] = low_ref[:, columns].astype(jnp.float32)
        wide[chunk, edge : edge + frames] = tokens_ref[:, columns].astype(jnp.float32)
        wide[chunk, edge + frames :] = high_ref[:, columns].astype(jnp.float32)
    block = 64

    @pl.loop(0, frames // block)
    def _(step):
        start = pl.multiple_of(step * block, block)
        for chunk in range(features // lanes):
            columns = slice(chunk * lanes, (chunk + 1) * lanes)
            filtered = None
            for k in range(taps):
                shifted = wide[chunk, pl.ds(start + (edge - taps // 2 + k), block), :]
                term = taps_ref[k : k + 1, columns] * shifted
                filtered = term if filtered is None else filtered + term
            middle = wide[chunk, pl.ds(start + edge, block), :]
            held[pl.ds(start, block), columns] = middle + filtered * jax.nn.sigmoid(filtered)

        stream = held[pl.ds(start, block), :].astype(jnp.bfloat16)
        stream_ref[pl.ds(start, block), :] = stream
        pack_ref[pl.ds(start, block), :] = layer_norm(stream, gain_ref[...])

    mask = jnp.broadcast_to(mask_ref[...].astype(jnp.float32), (MASK_ROWS, frames))
    pack_ref[frames:, :frames] = mask.astype(jnp.bfloat16)
    pack_ref[frames:, frames:] = jnp.zeros((MASK_ROWS, features - frames), jnp.bfloat16)


def tokens_part(tokens, low, high, mask, taps, gain):
    frames, features = tokens.shape
    edge = low.shape[0]
    return pl.pallas_call(
        tokens_kernel,
        out_shape=(
            jax.ShapeDtypeStruct((frames, features), jnp.bfloat16),
            jax.ShapeDtypeStruct((frames + MASK_ROWS, features), jnp.bfloat16),
        ),
        scratch_shapes=[
            pltpu.VMEM((features // 128, frames + 2 * edge, 128), jnp.float32),
            pltpu.VMEM((frames, features), jnp.float32),
        ],
        compiler_params=pltpu.CompilerParams(vmem_limit_bytes=48 * 1024 * 1024),
        cost_estimate=pl.CostEstimate(flops=8_000_000, bytes_accessed=1_500_000, transcendentals=0),
        name="tokens_part",
    )(tokens, low, high, mask, taps, gain)


def hidden_kernel(
    packs_ref, cotangents_ref, whole_ref, grad_ref, both_ref, up, delta, masked
):
    blocks, frames, features = cotangents_ref.shape
    hidden_ref, down_ref = both_ref.at[: blocks * frames], both_ref.at[blocks * frames :]
    half = whole_ref.shape[2] // 2
    part = half // XL
    for xh in range(XH):
        for z in range(Z):
            for xl in range(XL):
                row = ((xh * XL + xl) * Z + z) * part
                up[row : row + part] = whole_ref[xh, z, xl * part : (xl + 1) * part]
            row = (z * XH + xh) * half
            down_ref[row : row + half] = whole_ref[xh, z, half:]
    lanes = 128
    for index in range(blocks):
        rows = slice(index * frames, (index + 1) * frames)
        mask = packs_ref[index, frames:, :frames][:1].astype(jnp.float32)
        mask = jnp.broadcast_to(mask, (lanes, frames)).T
        for chunk in range(features // lanes):
            columns = slice(chunk * lanes, (chunk + 1) * lanes)
            kept = cotangents_ref[index, :, columns].astype(jnp.float32) * mask
            masked[:, columns] = kept.astype(jnp.bfloat16)
        normed = packs_ref[index, :frames]
        projected = jnp.dot(normed, up[...], preferred_element_type=jnp.float32)
        upstream = lax.dot_general(
            masked[...],
            down_ref[...],
            (((1,), (1,)), ((), ())),
            preferred_element_type=jnp.float32,
        )
        squashed = jax.nn.sigmoid(projected)
        hidden_ref[rows] = (projected * squashed).astype(jnp.bfloat16)
        delta[rows] = (0.5 * upstream * squashed * (1.0 + projected * (1.0 - squashed))).astype(
            jnp.bfloat16
        )
    total = None
    for index in range(blocks):
        rows = slice(index * frames, (index + 1) * frames)
        term = lax.dot_general(
            packs_ref[index, :frames],
            delta[rows],
            (((0,), (0,)), ((), ())),
            preferred_element_type=jnp.float32,
        )
        total = term if total is None else total + term
    grad_ref[...] = total.astype(jnp.bfloat16)


def hidden_part(packs, cotangents, whole):
    blocks, frames, features = cotangents.shape
    quarter = whole.shape[3]
    bf16 = jnp.bfloat16
    return pl.pallas_call(
        hidden_kernel,
        out_shape=(
            jax.ShapeDtypeStruct((features, quarter), bf16),
            jax.ShapeDtypeStruct((blocks * frames + quarter, features), bf16),
        ),
        scratch_shapes=[
            pltpu.VMEM((features, quarter), bf16),
            pltpu.VMEM((blocks * frames, quarter), bf16),
            pltpu.VMEM((frames, features), bf16),
        ],
        compiler_params=pltpu.CompilerParams(vmem_limit_bytes=16 * 1024 * 1024),
        name="hidden_part",
    )(packs, cotangents, whole)


def group_frames(block, x_block):
    pair = jnp.stack([block, x_block])
    return jnp.concatenate([pair, swap(pair, "c")])


def gather_by_exchange(block, axis):
    copies = jnp.broadcast_to(block[None], (lax.axis_size(axis), *block.shape))
    return lax.all_to_all(copies, axis, 0, 0, tiled=True)


def quarter_block(up_weight, down_weight):
    rows, hidden = up_weight.shape
    quarter = hidden // QUARTERS
    down_rows, features = down_weight.shape
    moves = []
    for q in range(QUARTERS):
        for z in range(Z):
            for c in range(C):
                source = (q * Z + z) * C + c
                target = ((c * XL + q // C) * Z + z) * C + q % C
                moves.append((source, target))
    down_block = lax.ppermute(down_weight, SEQ, moves)
    up_split = up_weight.reshape(rows, QUARTERS, quarter).transpose(1, 0, 2)
    up_block = lax.all_to_all(up_split, GROUP, 0, 0, tiled=True).reshape(QUARTERS * rows, quarter)
    return jnp.concatenate([up_block, down_block], axis=0)


def rows_kernel(pieces_ref, error_ref, start_ref, message_ref, memory_ref):
    chips, rows, quarter = pieces_ref.shape
    for xl in range(XL):
        total = None
        for chip in range(chips):
            if chip // Z % XL == xl:
                piece = pieces_ref[chip].astype(jnp.float32)
                total = piece if total is None else total + piece
        columns = slice(xl * quarter, (xl + 1) * quarter)
        memory_ref[:, columns] = total + error_ref[:, columns]
    memory = memory_ref[...]
    left = lax.dot_general(
        memory,
        start_ref[...],
        (((1,), (1,)), ((), ())),
        precision=HIGHEST,
        preferred_element_type=jnp.float32,
    )
    chunks, _, width = message_ref.shape
    part = width // C
    high = left.astype(jnp.bfloat16)
    low = (left - high.astype(jnp.float32)).astype(jnp.bfloat16)
    kept = memory.astype(jnp.bfloat16)
    for chunk in range(chunks):
        columns = slice(chunk * part, (chunk + 1) * part)
        message_ref[chunk] = jnp.concatenate([kept[:, columns], high, low], axis=1)


def rows_part(pieces, error_rows, start):
    rows, columns = error_rows.shape
    chunks = Y * C
    return pl.pallas_call(
        rows_kernel,
        out_shape=(
            jax.ShapeDtypeStruct((chunks, rows, C * columns // chunks), jnp.bfloat16),
            jax.ShapeDtypeStruct((rows, columns), jnp.float32),
        ),
        compiler_params=pltpu.CompilerParams(vmem_limit_bytes=8 * 1024 * 1024),
        name="rows_part",
    )(pieces, error_rows, start)


def mean_kernel(arrived_ref, message_ref):
    senders, rows, width = arrived_ref.shape
    part = width // C
    sums = []
    for c in range(C):
        total = arrived_ref[c].astype(jnp.float32)
        for sender in range(c + C, senders, C):
            total = total + arrived_ref[sender].astype(jnp.float32)
        sums.append(total / Y)
    left = sum(total[:, part : part + RANK] + total[:, part + RANK :] for total in sums)
    parts = [jnp.concatenate([total[:, :part] for total in sums], axis=1).astype(jnp.bfloat16)]
    for _ in range(3):
        parts.append(left.astype(jnp.bfloat16))
        left = left - parts[-1].astype(jnp.float32)
    parts.append(jnp.zeros((rows, width - 3 * RANK), jnp.bfloat16))
    row = jnp.concatenate(parts, axis=1)
    for chip in range(message_ref.shape[0]):
        message_ref[chip] = row


def mean_part(arrived, chips):
    _, rows, width = arrived.shape
    return pl.pallas_call(
        mean_kernel,
        out_shape=jax.ShapeDtypeStruct((chips, rows, 2 * width), jnp.bfloat16),
        compiler_params=pltpu.CompilerParams(vmem_limit_bytes=8 * 1024 * 1024),
        name="mean_part",
    )(arrived)


def last_kernel(arrived_ref, memory_ref, new_ref, compressed_ref):
    chunks, rows, width = arrived_ref.shape
    part = width // C
    per_quarter = chunks // XL
    for xl in range(XL):
        for c in range(C):
            mine = slice(c * part, (c + 1) * part)
            pieces = [arrived_ref[xl * per_quarter + k][:, mine] for k in range(per_quarter)]
            compressed = jnp.concatenate(pieces, axis=1)
            quarter = per_quarter * part
            columns = slice((xl * C + c) * quarter, (xl * C + c + 1) * quarter)
            compressed_ref[:, columns] = compressed
            new_ref[:, columns] = memory_ref[c, :, xl * quarter : (xl + 1) * quarter] - compressed


def last_part(arrived, memory_rows):
    _, rows, columns = memory_rows.shape
    shape = jax.ShapeDtypeStruct((rows, C * columns), jnp.float32)
    return pl.pallas_call(
        last_kernel,
        out_shape=(shape, shape),
        compiler_params=pltpu.CompilerParams(vmem_limit_bytes=8 * 1024 * 1024),
        name="last_part",
    )(arrived, memory_rows)


def by_core(mine, theirs, axis=0):
    first = lax.axis_index("c") == 0
    return jnp.concatenate(
        [jnp.where(first, mine, theirs), jnp.where(first, theirs, mine)], axis=axis
    )


def tail_kernel(chip_ref, columns_ref, message_ref, rows_scratch):
    chunks, rows, width = message_ref.shape
    rank = RANK
    terms = columns_ref[:, width:].astype(jnp.float32).T
    left_t = terms[:rank] + terms[rank : 2 * rank] + terms[2 * rank : 3 * rank]
    gram = lax.dot_general(
        left_t,
        left_t,
        (((1,), (1,)), ((), ())),
        precision=HIGHEST,
        preferred_element_type=jnp.float32,
    )
    index = lax.broadcasted_iota(jnp.int32, (rank, rank), 0)
    diagonal = index == lax.broadcasted_iota(jnp.int32, (rank, rank), 1)
    pivots = jnp.sum(jnp.where(diagonal, gram, 0.0), axis=1, keepdims=True)
    pivots = jnp.broadcast_to(pivots, (rank, width))
    gram = jnp.concatenate([gram, jnp.zeros((rank, width - rank), jnp.float32)], axis=1)
    row_index = lax.broadcasted_iota(jnp.int32, (rank, width), 0)
    parts = [left_t[:, at : at + width] for at in range(0, left_t.shape[1], width)]
    for k in range(rank):
        scale = lax.rsqrt(pivots[k : k + 1, :])
        column = jnp.broadcast_to(gram[:, k : k + 1], (rank, width))
        factor = jnp.where(row_index > k, column * scale, 0.0)
        gram = gram - factor * (gram[k : k + 1, :] * scale)
        solved_rows = [part[k : k + 1, :] * scale for part in parts]
        parts = [
            jnp.where(row_index == k, row, part - factor * row)
            for part, row in zip(parts, solved_rows)
        ]
        pivots = pivots - factor * factor
    solved = jnp.concatenate(parts, axis=1)
    rest, pieces = solved, []
    for _ in range(3):
        pieces.append(rest.astype(jnp.bfloat16))
        rest = rest - pieces[-1].astype(jnp.float32)
    products = jnp.dot(
        jnp.concatenate(pieces, axis=0),
        columns_ref[:, :width],
        preferred_element_type=jnp.float32,
    )
    right_t = products[:rank] + products[rank : 2 * rank] + products[2 * rank :]
    rows_scratch[...] = solved.T
    chip_rows = C * rows
    basis_rows = rows_scratch[pl.ds(pl.multiple_of(chip_ref[0] * chip_rows, chip_rows), chip_rows), :]
    piece = jnp.dot(basis_rows, right_t, precision=HIGHEST, preferred_element_type=jnp.float32)
    for chunk in range(chunks):
        half = chunk % C
        message_ref[chunk] = piece[half * rows : (half + 1) * rows]


def tail(chip, columns, chunks, rows, width):
    features = columns.shape[0]
    return pl.pallas_call(
        tail_kernel,
        out_shape=jax.ShapeDtypeStruct((chunks, rows, width), jnp.float32),
        in_specs=[
            pl.BlockSpec(memory_space=pltpu.SMEM),
            pl.BlockSpec(memory_space=pltpu.VMEM),
        ],
        out_specs=pl.BlockSpec(memory_space=pltpu.VMEM),
        scratch_shapes=[pltpu.VMEM((features, RANK), jnp.float32)],
        compiler_params=pltpu.CompilerParams(vmem_limit_bytes=8 * 1024 * 1024),
        name="tail",
    )(chip, columns)


def per_device(
    tokens,
    cotangent,
    up_weight,
    down_weight,
    kernel,
    norm_gain,
    frame_mask,
    error_memory,
    seed_matrix,
):
    frames, features = tokens.shape[1:]
    cotangent_x = swap(cotangent[0], "xl")
    low, high = halo(tokens[0], 16)
    block = quarter_block(up_weight, down_weight)
    block, low, high, cotangent_x = lax.optimization_barrier((block, low, high, cotangent_x))
    whole = gather_by_exchange(block, GROUPS).reshape(XH, Z, *block.shape)
    stream, own = tokens_part(tokens[0], low, high, frame_mask, kernel, norm_gain[None])
    packs = group_frames(own, swap(own, "xl"))
    cotangents = group_frames(cotangent[0], cotangent_x)
    grad_part, both = hidden_part(packs, cotangents, whole)

    hidden, down = both[: QUARTERS * frames], both[QUARTERS * frames :]
    mixed_part = jnp.dot(hidden, down, preferred_element_type=jnp.float32)
    mixed_part = mixed_part.reshape(C, XL, frames, features)
    mixed_away, error = lax.optimization_barrier((mixed_part[1], error_memory[0]))
    chip_part = mixed_part[0] + swap(mixed_away, "c")

    core = lax.axis_index("c")
    rows, quarter = error.shape[0], error.shape[1] // QUARTERS
    error = error.reshape(rows, XL, C, quarter).transpose(2, 0, 1, 3)
    error = error.reshape(C, rows, XL * quarter)
    error_rows = by_core(
        lax.dynamic_index_in_dim(error, core, keepdims=False),
        swap(lax.dynamic_index_in_dim(error, 1 - core, keepdims=False), "c"),
    )
    start = (seed_matrix.astype(jnp.float32) / 128.0).T.reshape(RANK, XL, C, quarter)
    start = lax.dynamic_index_in_dim(start, core, axis=2, keepdims=False).reshape(RANK, -1)

    chips = XH * XL * Z
    chip_rows = C * rows
    pieces = lax.all_to_all(grad_part.reshape(chips, chip_rows, quarter), CHIP, 0, 0, tiled=True)
    message, memory = rows_part(pieces, error_rows, start)

    arrived = lax.all_to_all(message, ("y", "c"), 0, 0, tiled=True)
    other_chip = swap(chip_part[1].astype(jnp.bfloat16), "xl")
    mixed = (
        stream.astype(jnp.float32) + 0.5 * (chip_part[0] + other_chip.astype(jnp.float32))
    ).astype(jnp.bfloat16)
    memory = memory.reshape(C, rows, XL * quarter)
    memory_rows = by_core(
        lax.dynamic_index_in_dim(memory, core),
        swap(lax.dynamic_index_in_dim(memory, 1 - core), "c"),
    )
    packed = mean_part(arrived, chips)
    columns = lax.all_to_all(packed, CHIP, 0, 0, tiled=True).reshape(features, -1)
    chip = lax.axis_index(CHIP).astype(jnp.int32).reshape(1)
    width = arrived.shape[2]
    message = tail(chip, columns, Y * C, rows, width)
    arrived = lax.all_to_all(message, ("y", "c"), 0, 0, tiled=True)
    new_memory, compressed = last_part(arrived, memory_rows)
    return (mixed[None], new_memory[None], compressed)


def solution(mesh):
    fine = Mesh(mesh.devices.reshape(Y, XH, XL, Z, C), ("y", *SEQ))
    in_specs = (
        P("y", SEQ, None),
        P("y", SEQ, None),
        P(SEQ, None),
        P(SEQ, None),
        P(),
        P(),
        P("y", SEQ),
        P("y", SEQ, None),
        P(),
    )
    out_specs = (P("y", SEQ, None), P("y", SEQ, None), P(SEQ, None))
    return jax.shard_map(
        per_device, mesh=fine, in_specs=in_specs, out_specs=out_specs, check_vma=False
    )
```

```python
import jax
import jax.numpy as jnp
from jax import lax
from jax.experimental import pallas as pl
from jax.experimental.pallas import tpu as pltpu
from jax.sharding import Mesh
from jax.sharding import PartitionSpec as P

Y, XH, XL, Z, C = 8, 2, 2, 8, 2
RANK = 32
MASK_ROWS = 16
CHIP = ("xh", "xl", "z")
SEQ = ("xh", "xl", "z", "c")
GROUP = ("xl", "c")
GROUPS = ("xh", "z")
QUARTERS = XL * C
HIGHEST = lax.Precision.HIGHEST


def halo(block, width):
    count = XH * XL * Z * C
    forward = [(i, i + 1) for i in range(count - 1)]
    backward = [(target, source) for source, target in forward]
    low = lax.ppermute(block[block.shape[0] - width :], SEQ, forward)
    high = lax.ppermute(block[:width], SEQ, backward)
    return low, high


def swap(block, axis):
    return lax.ppermute(block, axis, [(0, 1), (1, 0)])


def layer_norm(stream, norm_gain):
    values = stream.astype(jnp.float32)
    center = jnp.mean(values, axis=1, keepdims=True)
    spread = jnp.mean((values - center) ** 2, axis=1, keepdims=True)
    return ((values - center) * lax.rsqrt(spread + 1e-05) * norm_gain).astype(jnp.bfloat16)


def tokens_kernel(
    tokens_ref, low_ref, high_ref, mask_ref, taps_ref, gain_ref, stream_ref, pack_ref, wide, held
):
    frames, features = tokens_ref.shape
    edge = low_ref.shape[0]
    taps = taps_ref.shape[0]
    lanes = wide.shape[2]
    for chunk in range(features // lanes):
        columns = slice(chunk * lanes, (chunk + 1) * lanes)
        wide[chunk, :edge] = low_ref[:, columns].astype(jnp.float32)
        wide[chunk, edge : edge + frames] = tokens_ref[:, columns].astype(jnp.float32)
        wide[chunk, edge + frames :] = high_ref[:, columns].astype(jnp.float32)
    block = 64

    @pl.loop(0, frames // block)
    def _(step):
        start = pl.multiple_of(step * block, block)
        for chunk in range(features // lanes):
            columns = slice(chunk * lanes, (chunk + 1) * lanes)
            filtered = None
            for k in range(taps):
                shifted = wide[chunk, pl.ds(start + (edge - taps // 2 + k), block), :]
                term = taps_ref[k : k + 1, columns] * shifted
                filtered = term if filtered is None else filtered + term
            middle = wide[chunk, pl.ds(start + edge, block), :]
            held[pl.ds(start, block), columns] = middle + filtered * jax.nn.sigmoid(filtered)

        stream = held[pl.ds(start, block), :].astype(jnp.bfloat16)
        stream_ref[pl.ds(start, block), :] = stream
        pack_ref[pl.ds(start, block), :] = layer_norm(stream, gain_ref[...])

    mask = jnp.broadcast_to(mask_ref[...].astype(jnp.float32), (MASK_ROWS, frames))
    pack_ref[frames:, :frames] = mask.astype(jnp.bfloat16)
    pack_ref[frames:, frames:] = jnp.zeros((MASK_ROWS, features - frames), jnp.bfloat16)


def tokens_part(tokens, low, high, mask, taps, gain):
    frames, features = tokens.shape
    edge = low.shape[0]
    return pl.pallas_call(
        tokens_kernel,
        out_shape=(
            jax.ShapeDtypeStruct((frames, features), jnp.bfloat16),
            jax.ShapeDtypeStruct((frames + MASK_ROWS, features), jnp.bfloat16),
        ),
        scratch_shapes=[
            pltpu.VMEM((features // 128, frames + 2 * edge, 128), jnp.float32),
            pltpu.VMEM((frames, features), jnp.float32),
        ],
        compiler_params=pltpu.CompilerParams(vmem_limit_bytes=48 * 1024 * 1024),
        cost_estimate=pl.CostEstimate(flops=8_000_000, bytes_accessed=1_500_000, transcendentals=0),
        name="tokens_part",
    )(tokens, low, high, mask, taps, gain)


def hidden_kernel(
    packs_ref, cotangents_ref, whole_ref, grad_ref, both_ref, up, delta, masked
):
    blocks, frames, features = cotangents_ref.shape
    hidden_ref, down_ref = both_ref.at[: blocks * frames], both_ref.at[blocks * frames :]
    half = whole_ref.shape[2] // 2
    part = half // XL
    for xh in range(XH):
        for z in range(Z):
            for xl in range(XL):
                row = ((xh * XL + xl) * Z + z) * part
                up[row : row + part] = whole_ref[xh, z, xl * part : (xl + 1) * part]
            row = (z * XH + xh) * half
            down_ref[row : row + half] = whole_ref[xh, z, half:]
    lanes = 128
    for index in range(blocks):
        rows = slice(index * frames, (index + 1) * frames)
        mask = packs_ref[index, frames:, :frames][:1].astype(jnp.float32)
        mask = jnp.broadcast_to(mask, (lanes, frames)).T
        for chunk in range(features // lanes):
            columns = slice(chunk * lanes, (chunk + 1) * lanes)
            kept = cotangents_ref[index, :, columns].astype(jnp.float32) * mask
            masked[:, columns] = kept.astype(jnp.bfloat16)
        normed = packs_ref[index, :frames]
        projected = jnp.dot(normed, up[...], preferred_element_type=jnp.float32)
        upstream = lax.dot_general(
            masked[...],
            down_ref[...],
            (((1,), (1,)), ((), ())),
            preferred_element_type=jnp.float32,
        )
        squashed = 0.5 + 0.5 * jnp.tanh(0.5 * projected)
        hidden = projected * squashed
        hidden_ref[rows] = hidden.astype(jnp.bfloat16)
        slope = squashed + hidden * (1.0 - squashed)
        delta[rows] = (0.5 * upstream * slope).astype(jnp.bfloat16)
    total = None
    for index in range(blocks):
        rows = slice(index * frames, (index + 1) * frames)
        term = lax.dot_general(
            packs_ref[index, :frames],
            delta[rows],
            (((0,), (0,)), ((), ())),
            preferred_element_type=jnp.float32,
        )
        total = term if total is None else total + term
    grad_ref[...] = total.astype(jnp.bfloat16)


def hidden_part(packs, cotangents, whole):
    blocks, frames, features = cotangents.shape
    quarter = whole.shape[3]
    bf16 = jnp.bfloat16
    return pl.pallas_call(
        hidden_kernel,
        out_shape=(
            jax.ShapeDtypeStruct((features, quarter), bf16),
            jax.ShapeDtypeStruct((blocks * frames + quarter, features), bf16),
        ),
        scratch_shapes=[
            pltpu.VMEM((features, quarter), bf16),
            pltpu.VMEM((blocks * frames, quarter), bf16),
            pltpu.VMEM((frames, features), bf16),
        ],
        compiler_params=pltpu.CompilerParams(vmem_limit_bytes=16 * 1024 * 1024),
        name="hidden_part",
    )(packs, cotangents, whole)


def group_frames(block, x_block):
    pair = jnp.stack([block, x_block])
    return jnp.concatenate([pair, swap(pair, "c")])


def gather_by_exchange(block, axis):
    copies = jnp.broadcast_to(block[None], (lax.axis_size(axis), *block.shape))
    return lax.all_to_all(copies, axis, 0, 0, tiled=True)


def quarter_block(up_weight, down_weight):
    rows, hidden = up_weight.shape
    quarter = hidden // QUARTERS
    down_rows, features = down_weight.shape
    moves = []
    for q in range(QUARTERS):
        for z in range(Z):
            for c in range(C):
                source = (q * Z + z) * C + c
                target = ((c * XL + q // C) * Z + z) * C + q % C
                moves.append((source, target))
    down_block = lax.ppermute(down_weight, SEQ, moves)
    up_split = up_weight.reshape(rows, QUARTERS, quarter).transpose(1, 0, 2)
    up_block = lax.all_to_all(up_split, GROUP, 0, 0, tiled=True).reshape(QUARTERS * rows, quarter)
    return jnp.concatenate([up_block, down_block], axis=0)


def rows_kernel(pieces_ref, error_ref, start_ref, message_ref, memory_ref):
    chips, rows, quarter = pieces_ref.shape
    for xl in range(XL):
        total = None
        for chip in range(chips):
            if chip // Z % XL == xl:
                piece = pieces_ref[chip].astype(jnp.float32)
                total = piece if total is None else total + piece
        columns = slice(xl * quarter, (xl + 1) * quarter)
        memory_ref[:, columns] = total + error_ref[:, columns]
    memory = memory_ref[...]
    left = lax.dot_general(
        memory,
        start_ref[...],
        (((1,), (1,)), ((), ())),
        precision=HIGHEST,
        preferred_element_type=jnp.float32,
    )
    chunks, _, width = message_ref.shape
    part = width // C
    high = left.astype(jnp.bfloat16)
    low = (left - high.astype(jnp.float32)).astype(jnp.bfloat16)
    kept = memory.astype(jnp.bfloat16)
    for chunk in range(chunks):
        columns = slice(chunk * part, (chunk + 1) * part)
        message_ref[chunk] = jnp.concatenate([kept[:, columns], high, low], axis=1)


def rows_part(pieces, error_rows, start):
    rows, columns = error_rows.shape
    chunks = Y * C
    return pl.pallas_call(
        rows_kernel,
        out_shape=(
            jax.ShapeDtypeStruct((chunks, rows, C * columns // chunks), jnp.bfloat16),
            jax.ShapeDtypeStruct((rows, columns), jnp.float32),
        ),
        compiler_params=pltpu.CompilerParams(vmem_limit_bytes=8 * 1024 * 1024),
        name="rows_part",
    )(pieces, error_rows, start)


def mean_kernel(arrived_ref, message_ref):
    senders, rows, width = arrived_ref.shape
    part = width // C
    sums = []
    for c in range(C):
        total = arrived_ref[c].astype(jnp.float32)
        for sender in range(c + C, senders, C):
            total = total + arrived_ref[sender].astype(jnp.float32)
        sums.append(total / Y)
    left = sum(total[:, part : part + RANK] + total[:, part + RANK :] for total in sums)
    parts = [jnp.concatenate([total[:, :part] for total in sums], axis=1).astype(jnp.bfloat16)]
    for _ in range(3):
        parts.append(left.astype(jnp.bfloat16))
        left = left - parts[-1].astype(jnp.float32)
    parts.append(jnp.zeros((rows, width - 3 * RANK), jnp.bfloat16))
    row = jnp.concatenate(parts, axis=1)
    for chip in range(message_ref.shape[0]):
        message_ref[chip] = row


def mean_part(arrived, chips):
    _, rows, width = arrived.shape
    return pl.pallas_call(
        mean_kernel,
        out_shape=jax.ShapeDtypeStruct((chips, rows, 2 * width), jnp.bfloat16),
        compiler_params=pltpu.CompilerParams(vmem_limit_bytes=8 * 1024 * 1024),
        name="mean_part",
    )(arrived)


def last_kernel(arrived_ref, memory_ref, new_ref, compressed_ref):
    chunks, rows, width = arrived_ref.shape
    part = width // C
    per_quarter = chunks // XL
    for xl in range(XL):
        for c in range(C):
            mine = slice(c * part, (c + 1) * part)
            pieces = [arrived_ref[xl * per_quarter + k][:, mine] for k in range(per_quarter)]
            compressed = jnp.concatenate(pieces, axis=1)
            quarter = per_quarter * part
            columns = slice((xl * C + c) * quarter, (xl * C + c + 1) * quarter)
            compressed_ref[:, columns] = compressed
            new_ref[:, columns] = memory_ref[c, :, xl * quarter : (xl + 1) * quarter] - compressed


def last_part(arrived, memory_rows):
    _, rows, columns = memory_rows.shape
    shape = jax.ShapeDtypeStruct((rows, C * columns), jnp.float32)
    return pl.pallas_call(
        last_kernel,
        out_shape=(shape, shape),
        compiler_params=pltpu.CompilerParams(vmem_limit_bytes=8 * 1024 * 1024),
        name="last_part",
    )(arrived, memory_rows)


def by_core(mine, theirs, axis=0):
    first = lax.axis_index("c") == 0
    return jnp.concatenate(
        [jnp.where(first, mine, theirs), jnp.where(first, theirs, mine)], axis=axis
    )


def tail_kernel(chip_ref, columns_ref, message_ref, rows_scratch):
    chunks, rows, width = message_ref.shape
    rank = RANK
    terms = columns_ref[:, width:].astype(jnp.float32).T
    left_t = terms[:rank] + terms[rank : 2 * rank] + terms[2 * rank : 3 * rank]
    gram = lax.dot_general(
        left_t,
        left_t,
        (((1,), (1,)), ((), ())),
        precision=HIGHEST,
        preferred_element_type=jnp.float32,
    )
    index = lax.broadcasted_iota(jnp.int32, (rank, rank), 0)
    diagonal = index == lax.broadcasted_iota(jnp.int32, (rank, rank), 1)
    pivots = jnp.sum(jnp.where(diagonal, gram, 0.0), axis=1, keepdims=True)
    pivots = jnp.broadcast_to(pivots, (rank, width))
    gram = jnp.concatenate([gram, jnp.zeros((rank, width - rank), jnp.float32)], axis=1)
    row_index = lax.broadcasted_iota(jnp.int32, (rank, width), 0)
    parts = [left_t[:, at : at + width] for at in range(0, left_t.shape[1], width)]
    for k in range(rank):
        scale = lax.rsqrt(pivots[k : k + 1, :])
        column = jnp.broadcast_to(gram[:, k : k + 1], (rank, width))
        factor = jnp.where(row_index > k, column * scale, 0.0)
        gram = gram - factor * (gram[k : k + 1, :] * scale)
        solved_rows = [part[k : k + 1, :] * scale for part in parts]
        parts = [
            jnp.where(row_index == k, row, part - factor * row)
            for part, row in zip(parts, solved_rows)
        ]
        pivots = pivots - factor * factor
    solved = jnp.concatenate(parts, axis=1)
    rest, pieces = solved, []
    for _ in range(3):
        pieces.append(rest.astype(jnp.bfloat16))
        rest = rest - pieces[-1].astype(jnp.float32)
    products = jnp.dot(
        jnp.concatenate(pieces, axis=0),
        columns_ref[:, :width],
        preferred_element_type=jnp.float32,
    )
    right_t = products[:rank] + products[rank : 2 * rank] + products[2 * rank :]
    rows_scratch[...] = solved.T
    chip_rows = C * rows
    basis_rows = rows_scratch[pl.ds(pl.multiple_of(chip_ref[0] * chip_rows, chip_rows), chip_rows), :]
    piece = jnp.dot(basis_rows, right_t, precision=HIGHEST, preferred_element_type=jnp.float32)
    for chunk in range(chunks):
        half = chunk % C
        message_ref[chunk] = piece[half * rows : (half + 1) * rows]


def tail(chip, columns, chunks, rows, width):
    features = columns.shape[0]
    return pl.pallas_call(
        tail_kernel,
        out_shape=jax.ShapeDtypeStruct((chunks, rows, width), jnp.float32),
        in_specs=[
            pl.BlockSpec(memory_space=pltpu.SMEM),
            pl.BlockSpec(memory_space=pltpu.VMEM),
        ],
        out_specs=pl.BlockSpec(memory_space=pltpu.VMEM),
        scratch_shapes=[pltpu.VMEM((features, RANK), jnp.float32)],
        compiler_params=pltpu.CompilerParams(vmem_limit_bytes=8 * 1024 * 1024),
        name="tail",
    )(chip, columns)


def per_device(
    tokens,
    cotangent,
    up_weight,
    down_weight,
    kernel,
    norm_gain,
    frame_mask,
    error_memory,
    seed_matrix,
):
    frames, features = tokens.shape[1:]
    cotangent_x = swap(cotangent[0], "xl")
    low, high = halo(tokens[0], 16)
    block = quarter_block(up_weight, down_weight)
    block, low, high, cotangent_x = lax.optimization_barrier((block, low, high, cotangent_x))
    whole = gather_by_exchange(block, GROUPS).reshape(XH, Z, *block.shape)
    stream, own = tokens_part(tokens[0], low, high, frame_mask, kernel, norm_gain[None])
    packs = group_frames(own, swap(own, "xl"))
    cotangents = group_frames(cotangent[0], cotangent_x)
    grad_part, both = hidden_part(packs, cotangents, whole)

    hidden, down = both[: QUARTERS * frames], both[QUARTERS * frames :]
    mixed_part = jnp.dot(hidden, down, preferred_element_type=jnp.float32)
    mixed_part = mixed_part.reshape(C, XL, frames, features)
    mixed_away, error = lax.optimization_barrier((mixed_part[1], error_memory[0]))
    chip_part = mixed_part[0] + swap(mixed_away, "c")

    core = lax.axis_index("c")
    rows, quarter = error.shape[0], error.shape[1] // QUARTERS
    error = error.reshape(rows, XL, C, quarter).transpose(2, 0, 1, 3)
    error = error.reshape(C, rows, XL * quarter)
    error_rows = by_core(
        lax.dynamic_index_in_dim(error, core, keepdims=False),
        swap(lax.dynamic_index_in_dim(error, 1 - core, keepdims=False), "c"),
    )
    start = (seed_matrix.astype(jnp.float32) / 128.0).T.reshape(RANK, XL, C, quarter)
    start = lax.dynamic_index_in_dim(start, core, axis=2, keepdims=False).reshape(RANK, -1)

    chips = XH * XL * Z
    chip_rows = C * rows
    pieces = lax.all_to_all(grad_part.reshape(chips, chip_rows, quarter), CHIP, 0, 0, tiled=True)
    message, memory = rows_part(pieces, error_rows, start)

    arrived = lax.all_to_all(message, ("y", "c"), 0, 0, tiled=True)
    other_chip = swap(chip_part[1].astype(jnp.bfloat16), "xl")
    mixed = (
        stream.astype(jnp.float32) + 0.5 * (chip_part[0] + other_chip.astype(jnp.float32))
    ).astype(jnp.bfloat16)
    memory = memory.reshape(C, rows, XL * quarter)
    memory_rows = by_core(
        lax.dynamic_index_in_dim(memory, core),
        swap(lax.dynamic_index_in_dim(memory, 1 - core), "c"),
    )
    packed = mean_part(arrived, chips)
    columns = lax.all_to_all(packed, CHIP, 0, 0, tiled=True).reshape(features, -1)
    chip = lax.axis_index(CHIP).astype(jnp.int32).reshape(1)
    width = arrived.shape[2]
    message = tail(chip, columns, Y * C, rows, width)
    arrived = lax.all_to_all(message, ("y", "c"), 0, 0, tiled=True)
    new_memory, compressed = last_part(arrived, memory_rows)
    return (mixed[None], new_memory[None], compressed)


def solution(mesh):
    fine = Mesh(mesh.devices.reshape(Y, XH, XL, Z, C), ("y", *SEQ))
    in_specs = (
        P("y", SEQ, None),
        P("y", SEQ, None),
        P(SEQ, None),
        P(SEQ, None),
        P(),
        P(),
        P("y", SEQ),
        P("y", SEQ, None),
        P(),
    )
    out_specs = (P("y", SEQ, None), P("y", SEQ, None), P(SEQ, None))
    return jax.shard_map(
        per_device, mesh=fine, in_specs=in_specs, out_specs=out_specs, check_vma=False
    )
```

```python
import jax
import jax.numpy as jnp
from jax import lax
from jax.experimental import pallas as pl
from jax.experimental.pallas import tpu as pltpu
from jax.sharding import Mesh
from jax.sharding import PartitionSpec as P

Y, XH, XL, Z, C = 8, 2, 2, 8, 2
RANK = 32
MASK_ROWS = 16
CHIP = ("xh", "xl", "z")
SEQ = ("xh", "xl", "z", "c")
GROUP = ("xl", "c")
GROUPS = ("xh", "z")
QUARTERS = XL * C
HIGHEST = lax.Precision.HIGHEST


def halo(block, width):
    count = XH * XL * Z * C
    forward = [(i, i + 1) for i in range(count - 1)]
    backward = [(target, source) for source, target in forward]
    low = lax.ppermute(block[block.shape[0] - width :], SEQ, forward)
    high = lax.ppermute(block[:width], SEQ, backward)
    return low, high


def swap(block, axis):
    return lax.ppermute(block, axis, [(0, 1), (1, 0)])


def layer_norm(stream, norm_gain):
    values = stream.astype(jnp.float32)
    center = jnp.mean(values, axis=1, keepdims=True)
    spread = jnp.mean((values - center) ** 2, axis=1, keepdims=True)
    return ((values - center) * lax.rsqrt(spread + 1e-05) * norm_gain).astype(jnp.bfloat16)


def tokens_kernel(
    tokens_ref, low_ref, high_ref, mask_ref, taps_ref, gain_ref, stream_ref, pack_ref, wide, held
):
    frames, features = tokens_ref.shape
    edge = low_ref.shape[0]
    taps = taps_ref.shape[0]
    lanes = wide.shape[2]
    for chunk in range(features // lanes):
        columns = slice(chunk * lanes, (chunk + 1) * lanes)
        wide[chunk, :edge] = low_ref[:, columns].astype(jnp.float32)
        wide[chunk, edge : edge + frames] = tokens_ref[:, columns].astype(jnp.float32)
        wide[chunk, edge + frames :] = high_ref[:, columns].astype(jnp.float32)
    block = 64

    @pl.loop(0, frames // block)
    def _(step):
        start = pl.multiple_of(step * block, block)
        for chunk in range(features // lanes):
            columns = slice(chunk * lanes, (chunk + 1) * lanes)
            filtered = None
            for k in range(taps):
                shifted = wide[chunk, pl.ds(start + (edge - taps // 2 + k), block), :]
                term = taps_ref[k : k + 1, columns] * shifted
                filtered = term if filtered is None else filtered + term
            middle = wide[chunk, pl.ds(start + edge, block), :]
            held[pl.ds(start, block), columns] = middle + filtered * jax.nn.sigmoid(filtered)

        stream = held[pl.ds(start, block), :].astype(jnp.bfloat16)
        stream_ref[pl.ds(start, block), :] = stream
        pack_ref[pl.ds(start, block), :] = layer_norm(stream, gain_ref[...])

    mask = jnp.broadcast_to(mask_ref[...].astype(jnp.float32), (MASK_ROWS, frames))
    pack_ref[frames:, :frames] = mask.astype(jnp.bfloat16)
    pack_ref[frames:, frames:] = jnp.zeros((MASK_ROWS, features - frames), jnp.bfloat16)


def tokens_part(tokens, low, high, mask, taps, gain):
    frames, features = tokens.shape
    edge = low.shape[0]
    return pl.pallas_call(
        tokens_kernel,
        out_shape=(
            jax.ShapeDtypeStruct((frames, features), jnp.bfloat16),
            jax.ShapeDtypeStruct((frames + MASK_ROWS, features), jnp.bfloat16),
        ),
        scratch_shapes=[
            pltpu.VMEM((features // 128, frames + 2 * edge, 128), jnp.float32),
            pltpu.VMEM((frames, features), jnp.float32),
        ],
        compiler_params=pltpu.CompilerParams(vmem_limit_bytes=48 * 1024 * 1024),
        cost_estimate=pl.CostEstimate(flops=8_000_000, bytes_accessed=1_500_000, transcendentals=0),
        name="tokens_part",
    )(tokens, low, high, mask, taps, gain)


def hidden_kernel(
    packs_ref, cotangents_ref, whole_ref, grad_ref, both_ref, up, delta, masked
):
    blocks, frames, features = cotangents_ref.shape
    hidden_ref, down_ref = both_ref.at[: blocks * frames], both_ref.at[blocks * frames :]
    half = whole_ref.shape[2] // 2
    part = half // XL
    for xh in range(XH):
        for z in range(Z):
            for xl in range(XL):
                row = ((xh * XL + xl) * Z + z) * part
                up[row : row + part] = whole_ref[xh, z, xl * part : (xl + 1) * part]
            row = (z * XH + xh) * half
            down_ref[row : row + half] = whole_ref[xh, z, half:]
    lanes = 128
    for index in range(blocks):
        rows = slice(index * frames, (index + 1) * frames)
        mask = packs_ref[index, frames:, :frames][:1].astype(jnp.float32)
        mask = jnp.broadcast_to(mask, (lanes, frames)).T.astype(jnp.bfloat16)
        for chunk in range(features // lanes):
            columns = slice(chunk * lanes, (chunk + 1) * lanes)
            masked[:, columns] = cotangents_ref[index, :, columns] * mask
        normed = packs_ref[index, :frames]
        projected = jnp.dot(normed, up[...], preferred_element_type=jnp.float32)
        upstream = lax.dot_general(
            masked[...],
            down_ref[...],
            (((1,), (1,)), ((), ())),
            preferred_element_type=jnp.float32,
        )
        squashed = 0.5 + 0.5 * jnp.tanh(0.5 * projected)
        hidden = projected * squashed
        hidden_ref[rows] = hidden.astype(jnp.bfloat16)
        slope = squashed + hidden * (1.0 - squashed)
        delta[rows] = (0.5 * upstream * slope).astype(jnp.bfloat16)
    total = None
    for index in range(blocks):
        rows = slice(index * frames, (index + 1) * frames)
        term = lax.dot_general(
            packs_ref[index, :frames],
            delta[rows],
            (((0,), (0,)), ((), ())),
            preferred_element_type=jnp.float32,
        )
        total = term if total is None else total + term
    grad_ref[...] = total.astype(jnp.bfloat16)


def hidden_part(packs, cotangents, whole):
    blocks, frames, features = cotangents.shape
    quarter = whole.shape[3]
    bf16 = jnp.bfloat16
    return pl.pallas_call(
        hidden_kernel,
        out_shape=(
            jax.ShapeDtypeStruct((features, quarter), bf16),
            jax.ShapeDtypeStruct((blocks * frames + quarter, features), bf16),
        ),
        scratch_shapes=[
            pltpu.VMEM((features, quarter), bf16),
            pltpu.VMEM((blocks * frames, quarter), bf16),
            pltpu.VMEM((frames, features), bf16),
        ],
        compiler_params=pltpu.CompilerParams(vmem_limit_bytes=16 * 1024 * 1024),
        name="hidden_part",
    )(packs, cotangents, whole)


def group_frames(block, x_block):
    pair = jnp.stack([block, x_block])
    return jnp.concatenate([pair, swap(pair, "c")])


def gather_by_exchange(block, axis):
    copies = jnp.broadcast_to(block[None], (lax.axis_size(axis), *block.shape))
    return lax.all_to_all(copies, axis, 0, 0, tiled=True)


def quarter_block(up_weight, down_weight):
    rows, hidden = up_weight.shape
    quarter = hidden // QUARTERS
    down_rows, features = down_weight.shape
    moves = []
    for q in range(QUARTERS):
        for z in range(Z):
            for c in range(C):
                source = (q * Z + z) * C + c
                target = ((c * XL + q // C) * Z + z) * C + q % C
                moves.append((source, target))
    down_block = lax.ppermute(down_weight, SEQ, moves)
    up_split = up_weight.reshape(rows, QUARTERS, quarter).transpose(1, 0, 2)
    up_block = lax.all_to_all(up_split, GROUP, 0, 0, tiled=True).reshape(QUARTERS * rows, quarter)
    return jnp.concatenate([up_block, down_block], axis=0)


def rows_kernel(pieces_ref, error_ref, start_ref, message_ref, memory_ref):
    chips, rows, quarter = pieces_ref.shape
    for xl in range(XL):
        total = None
        for chip in range(chips):
            if chip // Z % XL == xl:
                piece = pieces_ref[chip].astype(jnp.float32)
                total = piece if total is None else total + piece
        columns = slice(xl * quarter, (xl + 1) * quarter)
        memory_ref[:, columns] = total + error_ref[:, columns]
    memory = memory_ref[...]
    left = lax.dot_general(
        memory,
        start_ref[...],
        (((1,), (1,)), ((), ())),
        precision=HIGHEST,
        preferred_element_type=jnp.float32,
    )
    chunks, _, width = message_ref.shape
    part = width // C
    high = left.astype(jnp.bfloat16)
    low = (left - high.astype(jnp.float32)).astype(jnp.bfloat16)
    kept = memory.astype(jnp.bfloat16)
    for chunk in range(chunks):
        columns = slice(chunk * part, (chunk + 1) * part)
        message_ref[chunk] = jnp.concatenate([kept[:, columns], high, low], axis=1)


def rows_part(pieces, error_rows, start):
    rows, columns = error_rows.shape
    chunks = Y * C
    return pl.pallas_call(
        rows_kernel,
        out_shape=(
            jax.ShapeDtypeStruct((chunks, rows, C * columns // chunks), jnp.bfloat16),
            jax.ShapeDtypeStruct((rows, columns), jnp.float32),
        ),
        compiler_params=pltpu.CompilerParams(vmem_limit_bytes=8 * 1024 * 1024),
        name="rows_part",
    )(pieces, error_rows, start)


def mean_kernel(arrived_ref, message_ref):
    senders, rows, width = arrived_ref.shape
    part = width // C
    sums = []
    for c in range(C):
        total = arrived_ref[c].astype(jnp.float32)
        for sender in range(c + C, senders, C):
            total = total + arrived_ref[sender].astype(jnp.float32)
        sums.append(total / Y)
    left = sum(total[:, part : part + RANK] + total[:, part + RANK :] for total in sums)
    parts = [jnp.concatenate([total[:, :part] for total in sums], axis=1).astype(jnp.bfloat16)]
    for _ in range(3):
        parts.append(left.astype(jnp.bfloat16))
        left = left - parts[-1].astype(jnp.float32)
    parts.append(jnp.zeros((rows, width - 3 * RANK), jnp.bfloat16))
    row = jnp.concatenate(parts, axis=1)
    for chip in range(message_ref.shape[0]):
        message_ref[chip] = row


def mean_part(arrived, chips):
    _, rows, width = arrived.shape
    return pl.pallas_call(
        mean_kernel,
        out_shape=jax.ShapeDtypeStruct((chips, rows, 2 * width), jnp.bfloat16),
        compiler_params=pltpu.CompilerParams(vmem_limit_bytes=8 * 1024 * 1024),
        name="mean_part",
    )(arrived)


def last_kernel(arrived_ref, memory_ref, new_ref, compressed_ref):
    chunks, rows, width = arrived_ref.shape
    part = width // C
    per_quarter = chunks // XL
    for xl in range(XL):
        for c in range(C):
            mine = slice(c * part, (c + 1) * part)
            pieces = [arrived_ref[xl * per_quarter + k][:, mine] for k in range(per_quarter)]
            compressed = jnp.concatenate(pieces, axis=1)
            quarter = per_quarter * part
            columns = slice((xl * C + c) * quarter, (xl * C + c + 1) * quarter)
            compressed_ref[:, columns] = compressed
            new_ref[:, columns] = memory_ref[c, :, xl * quarter : (xl + 1) * quarter] - compressed


def last_part(arrived, memory_rows):
    _, rows, columns = memory_rows.shape
    shape = jax.ShapeDtypeStruct((rows, C * columns), jnp.float32)
    return pl.pallas_call(
        last_kernel,
        out_shape=(shape, shape),
        compiler_params=pltpu.CompilerParams(vmem_limit_bytes=8 * 1024 * 1024),
        name="last_part",
    )(arrived, memory_rows)


def by_core(mine, theirs, axis=0):
    first = lax.axis_index("c") == 0
    return jnp.concatenate(
        [jnp.where(first, mine, theirs), jnp.where(first, theirs, mine)], axis=axis
    )


def tail_kernel(chip_ref, columns_ref, message_ref, rows_scratch):
    chunks, rows, width = message_ref.shape
    rank = RANK
    terms = columns_ref[:, width:].astype(jnp.float32).T
    left_t = terms[:rank] + terms[rank : 2 * rank] + terms[2 * rank : 3 * rank]
    gram = lax.dot_general(
        left_t,
        left_t,
        (((1,), (1,)), ((), ())),
        precision=HIGHEST,
        preferred_element_type=jnp.float32,
    )
    index = lax.broadcasted_iota(jnp.int32, (rank, rank), 0)
    diagonal = index == lax.broadcasted_iota(jnp.int32, (rank, rank), 1)
    pivots = jnp.sum(jnp.where(diagonal, gram, 0.0), axis=1, keepdims=True)
    pivots = jnp.broadcast_to(pivots, (rank, width))
    gram = jnp.concatenate([gram, jnp.zeros((rank, width - rank), jnp.float32)], axis=1)
    row_index = lax.broadcasted_iota(jnp.int32, (rank, width), 0)
    parts = [left_t[:, at : at + width] for at in range(0, left_t.shape[1], width)]
    for k in range(rank):
        scale = lax.rsqrt(pivots[k : k + 1, :])
        column = jnp.broadcast_to(gram[:, k : k + 1], (rank, width))
        factor = jnp.where(row_index > k, column * scale, 0.0)
        gram = gram - factor * (gram[k : k + 1, :] * scale)
        solved_rows = [part[k : k + 1, :] * scale for part in parts]
        parts = [
            jnp.where(row_index == k, row, part - factor * row)
            for part, row in zip(parts, solved_rows)
        ]
        pivots = pivots - factor * factor
    solved = jnp.concatenate(parts, axis=1)
    rest, pieces = solved, []
    for _ in range(3):
        pieces.append(rest.astype(jnp.bfloat16))
        rest = rest - pieces[-1].astype(jnp.float32)
    products = jnp.dot(
        jnp.concatenate(pieces, axis=0),
        columns_ref[:, :width],
        preferred_element_type=jnp.float32,
    )
    right_t = products[:rank] + products[rank : 2 * rank] + products[2 * rank :]
    rows_scratch[...] = solved.T
    chip_rows = C * rows
    basis_rows = rows_scratch[pl.ds(pl.multiple_of(chip_ref[0] * chip_rows, chip_rows), chip_rows), :]
    piece = jnp.dot(basis_rows, right_t, precision=HIGHEST, preferred_element_type=jnp.float32)
    for chunk in range(chunks):
        half = chunk % C
        message_ref[chunk] = piece[half * rows : (half + 1) * rows]


def tail(chip, columns, chunks, rows, width):
    features = columns.shape[0]
    return pl.pallas_call(
        tail_kernel,
        out_shape=jax.ShapeDtypeStruct((chunks, rows, width), jnp.float32),
        in_specs=[
            pl.BlockSpec(memory_space=pltpu.SMEM),
            pl.BlockSpec(memory_space=pltpu.VMEM),
        ],
        out_specs=pl.BlockSpec(memory_space=pltpu.VMEM),
        scratch_shapes=[pltpu.VMEM((features, RANK), jnp.float32)],
        compiler_params=pltpu.CompilerParams(vmem_limit_bytes=8 * 1024 * 1024),
        name="tail",
    )(chip, columns)


def per_device(
    tokens,
    cotangent,
    up_weight,
    down_weight,
    kernel,
    norm_gain,
    frame_mask,
    error_memory,
    seed_matrix,
):
    frames, features = tokens.shape[1:]
    cotangent_x = swap(cotangent[0], "xl")
    low, high = halo(tokens[0], 16)
    block = quarter_block(up_weight, down_weight)
    block, low, high, cotangent_x = lax.optimization_barrier((block, low, high, cotangent_x))
    whole = gather_by_exchange(block, GROUPS).reshape(XH, Z, *block.shape)
    stream, own = tokens_part(tokens[0], low, high, frame_mask, kernel, norm_gain[None])
    packs = group_frames(own, swap(own, "xl"))
    cotangents = group_frames(cotangent[0], cotangent_x)
    grad_part, both = hidden_part(packs, cotangents, whole)

    hidden, down = both[: QUARTERS * frames], both[QUARTERS * frames :]
    mixed_part = jnp.dot(hidden, down, preferred_element_type=jnp.float32)
    mixed_part = mixed_part.reshape(C, XL, frames, features)
    mixed_away, error = lax.optimization_barrier((mixed_part[1], error_memory[0]))
    chip_part = mixed_part[0] + swap(mixed_away, "c")

    core = lax.axis_index("c")
    rows, quarter = error.shape[0], error.shape[1] // QUARTERS
    error = error.reshape(rows, XL, C, quarter).transpose(2, 0, 1, 3)
    error = error.reshape(C, rows, XL * quarter)
    error_rows = by_core(
        lax.dynamic_index_in_dim(error, core, keepdims=False),
        swap(lax.dynamic_index_in_dim(error, 1 - core, keepdims=False), "c"),
    )
    start = (seed_matrix.astype(jnp.float32) / 128.0).T.reshape(RANK, XL, C, quarter)
    start = lax.dynamic_index_in_dim(start, core, axis=2, keepdims=False).reshape(RANK, -1)

    chips = XH * XL * Z
    chip_rows = C * rows
    pieces = lax.all_to_all(grad_part.reshape(chips, chip_rows, quarter), CHIP, 0, 0, tiled=True)
    message, memory = rows_part(pieces, error_rows, start)

    arrived = lax.all_to_all(message, ("y", "c"), 0, 0, tiled=True)
    other_chip = swap(chip_part[1].astype(jnp.bfloat16), "xl")
    mixed = (
        stream.astype(jnp.float32) + 0.5 * (chip_part[0] + other_chip.astype(jnp.float32))
    ).astype(jnp.bfloat16)
    memory = memory.reshape(C, rows, XL * quarter)
    memory_rows = by_core(
        lax.dynamic_index_in_dim(memory, core),
        swap(lax.dynamic_index_in_dim(memory, 1 - core), "c"),
    )
    packed = mean_part(arrived, chips)
    columns = lax.all_to_all(packed, CHIP, 0, 0, tiled=True).reshape(features, -1)
    chip = lax.axis_index(CHIP).astype(jnp.int32).reshape(1)
    width = arrived.shape[2]
    message = tail(chip, columns, Y * C, rows, width)
    arrived = lax.all_to_all(message, ("y", "c"), 0, 0, tiled=True)
    new_memory, compressed = last_part(arrived, memory_rows)
    return (mixed[None], new_memory[None], compressed)


def solution(mesh):
    fine = Mesh(mesh.devices.reshape(Y, XH, XL, Z, C), ("y", *SEQ))
    in_specs = (
        P("y", SEQ, None),
        P("y", SEQ, None),
        P(SEQ, None),
        P(SEQ, None),
        P(),
        P(),
        P("y", SEQ),
        P("y", SEQ, None),
        P(),
    )
    out_specs = (P("y", SEQ, None), P("y", SEQ, None), P(SEQ, None))
    return jax.shard_map(
        per_device, mesh=fine, in_specs=in_specs, out_specs=out_specs, check_vma=False
    )
```
